256 devices in a mesh: fsdp: 4 (over x_hi, core), seq: 64 (over y, x_lo, z).
Axes of the slice: x: 4 (x_hi: 2, x_lo: 2; x = x_hi * 2 + x_lo), y: 4, z: 8, core: 2. Of those that a mesh axis runs over, the one named last changes fastest.
Arguments:
- tokens: bfloat16 [4, 16384, 2304], P('fsdp', 'seq'), may hold values from -6 to 6
- norm_gain: float32 [2304], replicated, may hold values from 0.5 to 1.5
- w_qkv: bfloat16 [3, 2304, 1152], P(None, 'seq', 'fsdp'), may hold values from -0.125 to 0.125
- q_gain: float32 [96], replicated, may hold values from 0.8 to 7, as said below
- k_gain: float32 [96], replicated, may hold values from 0.8 to 7, as said below
- img_blocks: int32 [4, 64], replicated, may hold values from 1 to 4, 128 in all within a row
- img_width: int32 [4, 64], replicated, may hold values from 8 to 32
Outputs:
- attended: bfloat16 [4, 16384, 1152], P('fsdp', 'seq')
The draws below stay inside these ranges and needn't reach their ends.
Inputs may be any that keep to these rules, and one draw needn't show every extreme that they name: `img_blocks`: row p lists the lengths, in blocks of 128 tokens, of the 64 images of pack p in order; they sum to 128, and the longest is 4 blocks. `q_gain`: the same for every head. `k_gain`: the same for every head.
All inputs are finite; a program needn't handle non-finite values.
Results may differ from the reference program's by a relative error of at most 0.0045.
The reference program's roundings to bfloat16 on the way count: a program that leaves them out, or rounds other values in their place, can miss the bound.
Values may be sent and summed in bfloat16 or wider, within the bound.
No kernel may reach another device: no remote copies, remote signals or barrier semaphores. Data moves between devices by JAX's collectives and lax.ppermute only.
A program may use at most 64 MiB of HBM per device.

```python
import math
import jax
import jax.numpy as jnp
import numpy as np
from jax import lax

D = 2304
HEAD = 96
HEADS = 12
BLOCK = 128
MAXB = 4
TOK_DEV = 256
PACKS = 4
SEQLEN = 16384
HW = 1152
NBLK = 128
NIMG = 64
REACH = 2
N_SEQ = 64


def draw_gain_common(key, salt):
    inner = jax.random.fold_in(key, salt)
    return jax.random.uniform(inner, (HEAD,), jnp.float32, 0.8, 1.3)


def draw_q_gain(key, part):
    return draw_gain_common(key, 11)


def draw_k_gain(key, part):
    return draw_gain_common(key, 23)


def set_ends(array, own_key, least, top_value):
    dims = array.shape
    place = [jax.random.randint(jax.random.fold_in(own_key, axis), (), 0, dims[axis]) for axis in range(len(dims))]
    array = array.at[tuple(place)].set(least)
    longest = dims.index(max(dims))
    place[longest] = (place[longest] + 1) % dims[longest]
    return array.at[tuple(place)].set(top_value)


def block_scale(key, shape, shards, least, top_value):
    loudness = 1.0
    for axis_at, parts in shards:
        heights = jax.random.uniform(jax.random.fold_in(jax.random.fold_in(key, 6), axis_at), (parts,), jnp.float32, least / len(shards), top_value / len(shards))
        loudness = loudness * jnp.repeat(jnp.exp(heights), shape[axis_at] // parts).reshape((-1,) + (1,) * (len(shape) - 1 - axis_at))
    return loudness


def profile(count, total, bound, lean):
    portions = [(1 << 20) // math.isqrt(grade ** lean) + 1 for grade in range(2, count + 1)]
    spare, counts = total - bound - (count - 1), [1] * (count - 1)
    while spare > 0:
        candidates = [i for i in range(count - 1) if counts[i] < bound]
        pool, budget = sum([portions[i] for i in candidates]), spare
        for i in candidates:
            addition = min(bound - counts[i], max(1, budget * portions[i] // pool), spare)
            counts[i] = counts[i] + addition
            spare = spare - addition
    return np.array([bound] + counts)


def uneven_parts(stream_key, number_of, total, most, lean):
    if number_of == 2:
        one = jax.random.randint(stream_key, (), max(1, total - most), min(most, total - 1) + 1)
        return jnp.stack([one, total - one])
    lengths = jnp.asarray(profile(number_of, total, most, lean), jnp.int32)
    pairs = (number_of - 1) // 2
    giver, receiver = lengths[1:1 + 2 * pairs:2], lengths[2:2 + 2 * pairs:2]
    room = jnp.minimum(giver - 1, most - receiver)
    passed = jax.random.randint(jax.random.fold_in(stream_key, 1), (pairs,), 0, 1 << 20) % (room + 1)
    lengths = lengths.at[1:1 + 2 * pairs:2].set(giver - passed).at[2:2 + 2 * pairs:2].set(receiver + passed)
    return lengths[jax.random.permutation(jax.random.fold_in(stream_key, 2), number_of)]


def bell_draw(key, shape, width, reach, pieces=(), kind=jnp.bfloat16):
    drawn = jax.random.normal(key, shape, jnp.float32) * width
    if len(pieces) > 0:
        drawn = block_scale(key, shape, pieces, -0.22, 0.18) * drawn
    return jnp.clip(drawn, min=-reach, max=reach).astype(kind)


def setup_inputs(seed: int = 0) -> dict:
    seeds = jax.random.split(jax.random.key(seed), 8)
    return {
        "tokens": bell_draw(seeds[0], (PACKS, SEQLEN, D), 1.0, 6.0, ((0, 4), (1, 64))),
        "norm_gain": jnp.clip(1.0 + 0.1 * jax.random.normal(seeds[1], (D,), jnp.float32), 0.5, 1.5),
        "w_qkv": bell_draw(seeds[2], (3, D, HW), D ** -0.5, 0.125, ((1, 64), (2, 4))),
        "q_gain": draw_q_gain(jax.random.fold_in(seeds[7], 71), 0),
        "k_gain": draw_k_gain(jax.random.fold_in(seeds[7], 71), 0),
        "img_blocks": jax.vmap(lambda own: uneven_parts(own, NIMG, NBLK, MAXB, 2))(jax.random.split(seeds[5], PACKS)).reshape((PACKS, NIMG)).astype(jnp.int32),
        "img_width": set_ends(jax.random.randint(seeds[6], (PACKS, NIMG), 8, 33), jax.random.fold_in(seeds[6], 1), 8, 32).astype(jnp.int32),
    }


eps_model = 1e-06

def rms_norm(values, gain):
    return values * lax.rsqrt(lax.optimization_barrier(jnp.mean(values * values, axis=-1, keepdims=True)) + eps_model) * gain

def locate(blocks, widths, where, seq_total):
    starts = (jnp.cumsum(blocks, dtype=jnp.int32) - blocks) * BLOCK
    inside = (where[:, None] >= starts[None, :]).astype(jnp.int32)
    segment = lax.optimization_barrier(jnp.sum(inside, axis=1, dtype=jnp.int32)) - 1
    onehot = (segment[:, None] == jnp.arange(blocks.shape[0], dtype=jnp.int32)[None, :]).astype(jnp.int32)
    begin = lax.optimization_barrier(jnp.sum(onehot * starts[None, :], axis=1, dtype=jnp.int32))
    across = jnp.maximum(lax.optimization_barrier(jnp.sum(onehot * widths[None, :], axis=1, dtype=jnp.int32)), 1)
    offset = where - begin
    valid = (where >= 0) & (where < seq_total)
    return (jnp.where(valid, segment, -1), offset // across, offset % across)

def rotate(values, angle):
    pairs = angle.shape[-1]
    cosine = jnp.cos(angle)[..., None, :]
    sine = jnp.sin(angle)[..., None, :]
    first = values[..., :pairs]
    second = values[..., pairs:]
    return jnp.concatenate([first * cosine - second * sine, second * cosine + first * sine], axis=-1)

def rotary(values, row_pos, col_pos):
    half = values.shape[-1] // 2
    pairs = half // 2
    freq = 10000.0 ** (-jnp.arange(pairs, dtype=jnp.float32) / pairs)
    row_angle = row_pos.astype(jnp.float32)[..., None] * freq
    col_angle = col_pos.astype(jnp.float32)[..., None] * freq
    return jnp.concatenate([rotate(values[..., :half], row_angle), rotate(values[..., half:], col_angle)], axis=-1)

def softmax_mix(queries, key_rows, value_rows, seg_query, seg_key):
    scores = jnp.einsum('thd,shd->hts', queries.astype(jnp.float32), key_rows.astype(jnp.float32)) * HEAD ** (-0.5)
    mask = (seg_query[:, None] == seg_key[None, :])[None]
    top = lax.optimization_barrier(jnp.max(jnp.where(mask, scores, -1e+30), axis=-1, keepdims=True))
    expo = jnp.exp(jnp.where(mask, scores - top, -1e+30))
    weights = (expo / lax.optimization_barrier(jnp.sum(expo, axis=-1, keepdims=True))).astype(jnp.bfloat16)
    return jnp.einsum('hts,shd->thd', weights.astype(jnp.float32), value_rows.astype(jnp.float32)).astype(jnp.bfloat16)

def one_pack(tokens, norm_gain, w_qkv, q_gain, k_gain, blocks, widths):
    normed = rms_norm(tokens.astype(jnp.float32), norm_gain).astype(jnp.bfloat16)
    where = jnp.arange(SEQLEN, dtype=jnp.int32)
    segment, row_pos, col_pos = locate(blocks, widths, where, SEQLEN)
    head_shape = (SEQLEN, HEADS, HEAD)
    queries = jnp.dot(normed, w_qkv[0], preferred_element_type=jnp.float32).reshape(head_shape)
    queries = rotary(rms_norm(queries, q_gain), row_pos, col_pos).astype(jnp.bfloat16)
    key_rows = jnp.dot(normed, w_qkv[1], preferred_element_type=jnp.float32).reshape(head_shape)
    key_rows = rotary(rms_norm(key_rows, k_gain), row_pos, col_pos).astype(jnp.bfloat16)
    value_rows = jnp.dot(normed, w_qkv[2], preferred_element_type=jnp.float32).reshape(head_shape).astype(jnp.bfloat16)
    margin = REACH * TOK_DEV
    window = (2 * REACH + 1) * TOK_DEV
    padding = ((margin, margin), (0, 0), (0, 0))
    key_pad = jnp.pad(key_rows, padding)
    value_pad = jnp.pad(value_rows, padding)
    seg_pad = jnp.pad(segment, (margin, margin), constant_values=-1)

    def block_out(index):
        start = (index * TOK_DEV).astype(jnp.int32)
        query_block = lax.dynamic_slice_in_dim(queries, start, TOK_DEV, 0)
        seg_block = lax.dynamic_slice_in_dim(segment, start, TOK_DEV, 0)
        key_block = lax.dynamic_slice_in_dim(key_pad, start, window, 0)
        value_block = lax.dynamic_slice_in_dim(value_pad, start, window, 0)
        seg_keys = lax.dynamic_slice_in_dim(seg_pad, start, window, 0)
        return softmax_mix(query_block, key_block, value_block, seg_block, seg_keys)
    mixed = lax.map(block_out, jnp.arange(N_SEQ, dtype=jnp.int32))
    return mixed.reshape(SEQLEN, HEADS * HEAD)

def reference(tokens, norm_gain, w_qkv, q_gain, k_gain, img_blocks, img_width):
    outputs = []
    for pack_index in range(PACKS):
        outputs.append(one_pack(tokens[pack_index], norm_gain, w_qkv, q_gain, k_gain, img_blocks[pack_index], img_width[pack_index]))
    return jnp.stack(outputs)
```

```python
import itertools

import jax
import jax.numpy as jnp
from jax import lax
from jax.experimental import pallas as pl
from jax.experimental.pallas import tpu as pltpu
from jax.sharding import Mesh
from jax.sharding import PartitionSpec as P

HEAD = 96
BLOCK = 128
EPS = 1e-06
LANES = 128
AXES = ("xh", "c", "y", "xl", "z")
SIZES = {"xh": 2, "c": 2, "y": 4, "xl": 2, "z": 8}
D = 2304
TOK = 256
REACH = 3 * BLOCK
WIN = TOK + 2 * REACH
THREE = 288
OTHERS = (1, -1, 2)


def move(value, where):
    pairs = []
    for place in itertools.product(*[range(SIZES[a]) for a in AXES]):
        target = where(dict(zip(AXES, place)))
        if target is None:
            continue
        source_at = target_at = 0
        for axis, coordinate in zip(AXES, place):
            source_at = source_at * SIZES[axis] + coordinate
            target_at = target_at * SIZES[axis] + target[axis]
        pairs.append((source_at, target_at))
    return lax.ppermute(value, AXES, pairs)


def along(axis, by):
    def where(place):
        if axis == "x":
            x = (place["xh"] * 2 + place["xl"] + by) % 4
            return {**place, "xh": x // 2, "xl": x % 2}
        return {**place, axis: (place[axis] + by) % SIZES[axis]}

    return where


def along_seq(by):
    def where(place):
        s = (place["y"] * 2 + place["xl"]) * 8 + place["z"] + by
        if not 0 <= s < 64:
            return None
        return {**place, "y": s // 16, "xl": s // 8 % 2, "z": s % 8}

    return where


def gather_ring(value, axis):
    return [value] + [move(value, along(axis, -by)) for by in OTHERS]


def gather_z(mine):
    z = lax.axis_index("z")
    ahead, behind = move(mine, along("z", -1)), move(mine, along("z", 1))
    three = jnp.stack([behind, mine, ahead])
    far_ahead, far_behind = move(three, along("z", -3)), move(three, along("z", 3))
    relative = jnp.concatenate([far_behind, three, far_ahead[:2]], axis=0)
    doubled = jnp.concatenate([relative, relative], axis=0)
    return lax.dynamic_slice_in_dim(doubled, (12 - z) % 8, 8, 0)


def attend_kernel(
    info, own, halo, table, gains, *refs
):
    pieces, (out, w_all, x_all, keys, values, results, w_sem, x_sem) = refs[:8], refs[8:]
    x_here, y_here = info[0], info[1]
    copies = []
    for half, group in enumerate((pieces[:4], pieces[4:])):
        for far, piece in enumerate(group):
            for near in range(4):
                by_near, by_far = ((0,) + OTHERS)[near], ((0,) + OTHERS)[far]
                dx, dy = (by_near, by_far) if half == 0 else (by_far, by_near)
                x_from = lax.rem(x_here + (dx + 4), 4)
                y_from = lax.rem(y_here + (dy + 4), 4)
                row = (2 * y_from + lax.rem(x_from, 2)) * 288 + half * 144
                column_half = lax.div(x_from, 2)
                pltpu.make_async_copy(
                    piece.at[near],
                    w_all.at[column_half, pl.ds(pl.multiple_of(row, 144), 144)],
                    w_sem.at[column_half],
                ).start()
    for source, at, rows in (
        (halo.at[pl.ds(0, REACH)], 0, REACH),
        (own, REACH, TOK),
        (halo.at[pl.ds(REACH, REACH)], REACH + TOK, REACH),
    ):
        copies.append(
            pltpu.make_async_copy(source, x_all.at[pl.ds(at, rows)], x_sem)
        )
        copies[-1].start()
    pltpu.make_async_copy(x_all, x_all, x_sem).wait()

    def unit(raw, gain):
        lane = lax.broadcasted_iota(jnp.int32, raw.shape, 1)
        raw = jnp.where(lane < HEAD, raw, 0.0)
        mean = jnp.sum(raw * raw, axis=1, keepdims=True) * (1.0 / HEAD)
        return raw * lax.rsqrt(mean + EPS) * gain

    def turn(value, cosine, sine):
        lane = lax.broadcasted_iota(jnp.int32, value.shape, 1)
        low = lax.rem(lane, 48) < 24
        partner = jnp.where(
            low, pltpu.roll(value, LANES - 24, 1), pltpu.roll(value, 24, 1)
        )
        return value * cosine + partner * sine

    for column_half in range(2):
        pltpu.make_async_copy(
            w_all.at[column_half], w_all.at[column_half], w_sem.at[column_half]
        ).wait()

        def project(step, carry):
            rows = pl.ds(pl.multiple_of(step * 256, 256), 256)
            raw = jnp.dot(
                x_all[rows], w_all[column_half, :, 0:640], preferred_element_type=jnp.float32
            )
            cosine, sine = table[0, rows], table[1, rows]
            for head in range(3):
                part = raw[:, HEAD * head : HEAD * head + LANES]
                keys[head, rows] = turn(unit(part, gains[1:2]), cosine, sine).astype(jnp.bfloat16)
                part = raw[:, THREE + HEAD * head : THREE + HEAD * head + LANES]
                values[head, rows] = part.astype(jnp.bfloat16)
            return carry

        lax.fori_loop(0, WIN // 256, project, 0)
        mine = pl.ds(REACH, TOK)
        raw = jnp.dot(
            x_all[mine], w_all[column_half, :, 512:864], preferred_element_type=jnp.float32
        )
        for head in range(3):
            at = 64 + HEAD * head
            part = raw[:, at : at + HEAD]
            part = jnp.concatenate([part, jnp.zeros((TOK, LANES - HEAD), jnp.float32)], axis=1)
            queries = turn(unit(part, gains[0:1]), table[0, mine], table[1, mine]).astype(jnp.bfloat16)
            for block in range(2):
                begin = pl.multiple_of(info[2 + 2 * block], BLOCK)
                reach = info[3 + 2 * block]
                window = pl.ds(begin, 4 * BLOCK)
                scores = lax.dot_general(
                    queries[BLOCK * block : BLOCK * (block + 1)],
                    keys[head, window],
                    (((1,), (1,)), ((), ())),
                    preferred_element_type=jnp.float32,
                ) * (HEAD ** (-0.5))
                column = lax.broadcasted_iota(jnp.int32, scores.shape, 1)
                scores = jnp.where(column < reach, scores, -1e30)
                expo = jnp.exp(scores - jnp.max(scores, axis=1, keepdims=True))
                probs = expo * (1.0 / jnp.sum(expo, axis=1, keepdims=True))
                mixed = jnp.dot(
                    probs.astype(jnp.bfloat16), values[head, window], preferred_element_type=jnp.float32
                )
                results[column_half * 3 + head, pl.ds(BLOCK * block, BLOCK)] = mixed
    out[...] = jnp.concatenate(
        [results[head][:, :HEAD] for head in range(6)], axis=1
    ).astype(jnp.bfloat16)


def attend(info, own, halo, table, gains, pieces):
    anywhere = pl.BlockSpec(memory_space=pl.ANY)
    vmem = pl.BlockSpec(memory_space=pltpu.VMEM)
    return pl.pallas_call(
        attend_kernel,
        out_shape=jax.ShapeDtypeStruct((TOK, 2 * THREE), jnp.bfloat16),
        in_specs=[pl.BlockSpec(memory_space=pltpu.SMEM), anywhere, anywhere, vmem, vmem] + [anywhere] * 8,
        out_specs=vmem,
        scratch_shapes=[
            pltpu.VMEM((2, D, 3 * THREE), jnp.bfloat16),
            pltpu.VMEM((WIN, D), jnp.bfloat16),
            pltpu.VMEM((3, WIN, LANES), jnp.bfloat16),
            pltpu.VMEM((3, WIN, LANES), jnp.bfloat16),
            pltpu.VMEM((6, TOK, LANES), jnp.float32),
            pltpu.SemaphoreType.DMA((2,)),
            pltpu.SemaphoreType.DMA,
        ],
        compiler_params=pltpu.CompilerParams(vmem_limit_bytes=40 * 2**20),
        cost_estimate=pl.CostEstimate(
            flops=2 * D * 864 * 2 * 1024, bytes_accessed=14 * 2**20, transcendentals=2**20
        ),
    )(info, own, halo, table, gains, *pieces)


def places(blocks, widths, shard):
    order = jnp.arange(64, dtype=jnp.int32)
    starts = jnp.sum(jnp.where(order[None, :] < order[:, None], blocks[None, :], 0), axis=1)
    block_at = shard * 2 - 3 + jnp.arange(8, dtype=jnp.int32)
    begun = starts[None, :] <= block_at[:, None]
    inside = begun & (block_at[:, None] < (starts + blocks)[None, :])
    begin = jnp.sum(jnp.where(inside, starts[None, :], 0), axis=1)
    length = jnp.sum(jnp.where(inside, blocks[None, :], 0), axis=1)
    across = jnp.maximum(jnp.sum(jnp.where(inside, widths[None, :], 0), axis=1), 1)
    offset = (block_at - begin)[:, None] * BLOCK + jnp.arange(BLOCK, dtype=jnp.int32)[None, :]
    row, column = lax.div(offset, across[:, None] + 0 * offset), lax.rem(offset, across[:, None] + 0 * offset)
    back = (begin - block_at + jnp.arange(8, dtype=jnp.int32)) * BLOCK
    return row.reshape(WIN), column.reshape(WIN), back, length * BLOCK


def angles(row, column):
    lane = jnp.arange(LANES, dtype=jnp.int32)
    freq = 10000.0 ** (-(lane % 24).astype(jnp.float32) / 24)
    place = jnp.where(lane[None, :] < 48, row[:, None], column[:, None]).astype(jnp.float32)
    angle = place * freq[None, :]
    sign = jnp.where(lane % 48 < 24, -1.0, 1.0)
    real = lane < HEAD
    return jnp.stack(
        [jnp.where(real, jnp.cos(angle), 0.0), jnp.where(real, jnp.sin(angle) * sign, 0.0)]
    )


def shards(tokens, norm_gain, w_qkv, q_gain, k_gain, img_blocks, img_width):
    xh, core, y, xl, z = (lax.axis_index(a) for a in AXES)
    shard = (y * 2 + xl) * 8 + z
    mine = jnp.concatenate([w_qkv[1], w_qkv[2], w_qkv[0]], axis=1)
    rows = gather_z(mine).reshape(2, 144, 3 * THREE)
    first = jnp.stack(gather_ring(rows[0], "x"))
    second = jnp.stack(gather_ring(rows[1], "y"))
    pieces = gather_ring(first, "y") + gather_ring(second, "x")
    wide = tokens[0].astype(jnp.float32)
    scaled = wide * lax.rsqrt(jnp.mean(wide * wide, axis=-1, keepdims=True) + EPS) * norm_gain
    normed = scaled.astype(jnp.bfloat16)
    halo = jnp.concatenate(
        [
            move(normed[TOK - BLOCK :], along_seq(2)),
            move(normed, along_seq(1)),
            move(normed, along_seq(-1)),
            move(normed[:BLOCK], along_seq(-2)),
        ],
        axis=0,
    )
    normed_other = move(normed, along("c", 1))
    halo_other = move(halo, along("c", 1))
    gains = jnp.pad(jnp.stack([q_gain, k_gain]), ((0, 0), (0, LANES - HEAD)))

    def one(pack, own, around):
        blocks = lax.dynamic_slice_in_dim(img_blocks, pack, 1, 0)[0]
        widths = lax.dynamic_slice_in_dim(img_width, pack, 1, 0)[0]
        row, column, back, length = places(blocks, widths, shard)
        info = jnp.stack([xh * 2 + xl, y, back[3], length[3], back[4], length[4]]).astype(jnp.int32)
        return attend(info, own, around, angles(row, column), gains, pieces)

    theirs = one(xh * 2 + 1 - core, normed_other, halo_other)
    received = move(theirs, along("c", 1))
    ours = one(xh * 2 + core, normed, halo)
    left = jnp.where(core == 0, ours, received)
    right = jnp.where(core == 0, received, ours)
    whole = jnp.concatenate(
        [left[:, :THREE], right[:, :THREE], left[:, THREE:], right[:, THREE:]], axis=1
    )
    return whole[None]


def solution(mesh):
    devices = mesh.devices.reshape([SIZES[a] for a in AXES])
    fine = Mesh(devices, AXES)
    return jax.shard_map(
        shards,
        mesh=fine,
        in_specs=(
            P(("xh", "c"), ("y", "xl", "z"), None),
            P(),
            P(None, ("y", "xl", "z"), ("xh", "c")),
            P(),
            P(),
            P(),
            P(),
        ),
        out_specs=P(("xh", "c"), ("y", "xl", "z"), None),
        check_vma=False,
    )
```

```python
import functools
import itertools

import jax
import jax.numpy as jnp
from jax import lax
from jax.experimental import pallas as pl
from jax.experimental.pallas import tpu as pltpu
from jax.sharding import Mesh
from jax.sharding import PartitionSpec as P

HEAD = 96
BLOCK = 128
EPS = 1e-06
LANES = 128
AXES = ("xh", "c", "y", "xl", "z")
SIZES = {"xh": 2, "c": 2, "y": 4, "xl": 2, "z": 8}
D = 2304
TOK = 256
REACH = 3 * BLOCK
WIN = TOK + 2 * REACH
THREE = 288
OTHERS = (1, -1, 2)


def move(value, where):
    pairs = []
    for place in itertools.product(*[range(SIZES[a]) for a in AXES]):
        target = where(dict(zip(AXES, place)))
        if target is None:
            continue
        source_at = target_at = 0
        for axis, coordinate in zip(AXES, place):
            source_at = source_at * SIZES[axis] + coordinate
            target_at = target_at * SIZES[axis] + target[axis]
        pairs.append((source_at, target_at))
    return lax.ppermute(value, AXES, pairs)


def along(axis, by):
    def where(place):
        if axis == "x":
            x = (place["xh"] * 2 + place["xl"] + by) % 4
            return {**place, "xh": x // 2, "xl": x % 2}
        return {**place, axis: (place[axis] + by) % SIZES[axis]}

    return where


def along_seq(by):
    def where(place):
        s = (place["y"] * 2 + place["xl"]) * 8 + place["z"] + by
        if not 0 <= s < 64:
            return None
        return {**place, "y": s // 16, "xl": s // 8 % 2, "z": s % 8}

    return where


def mirrored(axis_move, by):
    def where(place):
        return axis_move(by if place["c"] == 0 else -by)(place)

    return where


def neighbours(value, axis):
    return move(value, along(axis, -1)), move(value, along(axis, 1))


def opposite(ahead, behind, axis, core):
    return move(jnp.where(core == 0, behind, ahead), mirrored(functools.partial(along, axis), 1))


def gather_z(mine):
    z = lax.axis_index("z")
    ahead, behind = move(mine, along("z", -1)), move(mine, along("z", 1))
    three = jnp.stack([behind, mine, ahead])
    far_ahead, far_behind = move(three, along("z", -3)), move(three, along("z", 3))
    relative = jnp.concatenate([far_behind, three, far_ahead[:2]], axis=0)
    doubled = jnp.concatenate([relative, relative], axis=0)
    return lax.dynamic_slice_in_dim(doubled, (12 - z) % 8, 8, 0)


def attend_kernel(info, table, gains, *refs):
    (own, side, back, far_side, far_back), refs = refs[:5], refs[5:]
    pieces, (out, w_all, x_all, keys, values, results, w_sem, x_sem) = refs[:8], refs[8:]
    x_here, y_here = info[0], info[1]
    for half, group in enumerate((pieces[:4], pieces[4:])):
        for far, piece in enumerate(group):
            for near in range(4):
                by_near, by_far = ((0,) + OTHERS)[near], ((0,) + OTHERS)[far]
                dx, dy = (by_near, by_far) if half == 0 else (by_far, by_near)
                x_from = lax.rem(x_here + (dx + 4), 4)
                y_from = lax.rem(y_here + (dy + 4), 4)
                row = (2 * y_from + lax.rem(x_from, 2)) * 288 + half * 144
                column_half = lax.div(x_from, 2)
                pltpu.make_async_copy(
                    piece.at[near],
                    w_all.at[column_half, pl.ds(pl.multiple_of(row, 144), 144)],
                    w_sem.at[column_half],
                ).start()
    flipped = info[6]
    left, right = BLOCK, REACH + TOK
    for source, at in (
        (own, REACH),
        (side, jnp.where(flipped == 0, left, right)),
        (back, jnp.where(flipped == 0, right, left)),
        (far_side, jnp.where(flipped == 0, 0, WIN - BLOCK)),
        (far_back, jnp.where(flipped == 0, WIN - BLOCK, 0)),
    ):
        rows = source.shape[0]
        pltpu.make_async_copy(source, x_all.at[pl.ds(pl.multiple_of(at, BLOCK), rows)], x_sem).start()
    pltpu.make_async_copy(x_all, x_all, x_sem).wait()

    def unit(raw, gain):
        lane = lax.broadcasted_iota(jnp.int32, raw.shape, 1)
        raw = jnp.where(lane < HEAD, raw, 0.0)
        mean = jnp.sum(raw * raw, axis=1, keepdims=True) * (1.0 / HEAD)
        return raw * lax.rsqrt(mean + EPS) * gain

    def turn(value, cosine, sine):
        lane = lax.broadcasted_iota(jnp.int32, value.shape, 1)
        low = lax.rem(lane, 48) < 24
        partner = jnp.where(
            low, pltpu.roll(value, LANES - 24, 1), pltpu.roll(value, 24, 1)
        )
        return value * cosine + partner * sine

    for column_half in range(2):
        pltpu.make_async_copy(
            w_all.at[column_half], w_all.at[column_half], w_sem.at[column_half]
        ).wait()

        def project(step, carry):
            rows = pl.ds(pl.multiple_of(step * 256, 256), 256)
            raw = jnp.dot(
                x_all[rows], w_all[column_half, :, 0:640], preferred_element_type=jnp.float32
            )
            cosine, sine = table[0, rows], table[1, rows]
            for head in range(3):
                part = raw[:, HEAD * head : HEAD * head + LANES]
                keys[head, rows] = turn(unit(part, gains[1:2]), cosine, sine).astype(jnp.bfloat16)
                part = raw[:, THREE + HEAD * head : THREE + HEAD * head + LANES]
                values[head, rows] = part.astype(jnp.bfloat16)
            return carry

        lax.fori_loop(0, WIN // 256, project, 0)
        mine = pl.ds(REACH, TOK)
        raw = jnp.dot(
            x_all[mine], w_all[column_half, :, 512:864], preferred_element_type=jnp.float32
        )
        for head in range(3):
            at = 64 + HEAD * head
            part = raw[:, at : at + HEAD]
            part = jnp.concatenate([part, jnp.zeros((TOK, LANES - HEAD), jnp.float32)], axis=1)
            queries = turn(unit(part, gains[0:1]), table[0, mine], table[1, mine]).astype(jnp.bfloat16)
            for block in range(2):
                begin = pl.multiple_of(info[2 + 2 * block], BLOCK)
                reach = info[3 + 2 * block]
                window = pl.ds(begin, 4 * BLOCK)
                scores = lax.dot_general(
                    queries[BLOCK * block : BLOCK * (block + 1)],
                    keys[head, window],
                    (((1,), (1,)), ((), ())),
                    preferred_element_type=jnp.float32,
                ) * (HEAD ** (-0.5))
                column = lax.broadcasted_iota(jnp.int32, scores.shape, 1)
                scores = jnp.where(column < reach, scores, -1e30)
                expo = jnp.exp(scores - jnp.max(scores, axis=1, keepdims=True))
                probs = expo * (1.0 / jnp.sum(expo, axis=1, keepdims=True))
                mixed = jnp.dot(
                    probs.astype(jnp.bfloat16), values[head, window], preferred_element_type=jnp.float32
                )
                results[column_half * 3 + head, pl.ds(BLOCK * block, BLOCK)] = mixed
    out[...] = jnp.concatenate(
        [results[head][:, :HEAD] for head in range(6)], axis=1
    ).astype(jnp.bfloat16)


def attend(info, tokens_of, table, gains, pieces):
    anywhere = pl.BlockSpec(memory_space=pl.ANY)
    vmem = pl.BlockSpec(memory_space=pltpu.VMEM)
    return pl.pallas_call(
        attend_kernel,
        out_shape=jax.ShapeDtypeStruct((TOK, 2 * THREE), jnp.bfloat16),
        in_specs=[pl.BlockSpec(memory_space=pltpu.SMEM), vmem, vmem] + [anywhere] * 13,
        out_specs=vmem,
        scratch_shapes=[
            pltpu.VMEM((2, D, 3 * THREE), jnp.bfloat16),
            pltpu.VMEM((WIN, D), jnp.bfloat16),
            pltpu.VMEM((3, WIN, LANES), jnp.bfloat16),
            pltpu.VMEM((3, WIN, LANES), jnp.bfloat16),
            pltpu.VMEM((6, TOK, LANES), jnp.float32),
            pltpu.SemaphoreType.DMA((2,)),
            pltpu.SemaphoreType.DMA,
        ],
        compiler_params=pltpu.CompilerParams(vmem_limit_bytes=60 * 2**20),
        cost_estimate=pl.CostEstimate(
            flops=2 * D * 864 * 2 * 1024, bytes_accessed=14 * 2**20, transcendentals=2**20
        ),
    )(info, table, gains, *tokens_of, *pieces)


def places(blocks, widths, shard):
    order = jnp.arange(64, dtype=jnp.int32)
    starts = jnp.sum(jnp.where(order[None, :] < order[:, None], blocks[None, :], 0), axis=1)
    block_at = shard * 2 - 3 + jnp.arange(8, dtype=jnp.int32)
    begun = starts[None, :] <= block_at[:, None]
    inside = begun & (block_at[:, None] < (starts + blocks)[None, :])
    begin = jnp.sum(jnp.where(inside, starts[None, :], 0), axis=1)
    length = jnp.sum(jnp.where(inside, blocks[None, :], 0), axis=1)
    across = jnp.maximum(jnp.sum(jnp.where(inside, widths[None, :], 0), axis=1), 1)
    offset = (block_at - begin)[:, None] * BLOCK + jnp.arange(BLOCK, dtype=jnp.int32)[None, :]
    row, column = lax.div(offset, across[:, None] + 0 * offset), lax.rem(offset, across[:, None] + 0 * offset)
    back = (begin - block_at + jnp.arange(8, dtype=jnp.int32)) * BLOCK
    return row.reshape(WIN), column.reshape(WIN), back, length * BLOCK


def angles(row, column):
    lane = jnp.arange(LANES, dtype=jnp.int32)
    freq = 10000.0 ** (-(lane % 24).astype(jnp.float32) / 24)
    place = jnp.where(lane[None, :] < 48, row[:, None], column[:, None]).astype(jnp.float32)
    angle = place * freq[None, :]
    sign = jnp.where(lane % 48 < 24, -1.0, 1.0)
    real = lane < HEAD
    return jnp.stack(
        [jnp.where(real, jnp.cos(angle), 0.0), jnp.where(real, jnp.sin(angle) * sign, 0.0)]
    )


def shards(tokens, norm_gain, w_qkv, q_gain, k_gain, img_blocks, img_width):
    xh, core, y, xl, z = (lax.axis_index(a) for a in AXES)
    shard = (y * 2 + xl) * 8 + z
    mine = jnp.concatenate([w_qkv[1], w_qkv[2], w_qkv[0]], axis=1)
    rows = gather_z(mine).reshape(2, 144, 3 * THREE)
    wide = tokens[0].astype(jnp.float32)
    scaled = wide * lax.rsqrt(jnp.mean(wide * wide, axis=-1, keepdims=True) + EPS) * norm_gain
    normed = scaled.astype(jnp.bfloat16)
    swap = functools.partial(move, where=along("c", 1))
    step_out, step_in = mirrored(along_seq, 1), mirrored(along_seq, -1)
    normed_other = swap(normed)
    rows, normed = lax.optimization_barrier((rows, normed))
    x_near, y_near = neighbours(rows[0], "x"), neighbours(rows[1], "y")
    side = move(normed, step_out)
    first = jnp.stack([rows[0], *x_near, opposite(*x_near, "x", core)])
    second = jnp.stack([rows[1], *y_near, opposite(*y_near, "y", core)])
    first, second, side, normed = lax.optimization_barrier((first, second, side, normed))
    side_other = swap(side)
    y_near, x_near = neighbours(first, "y"), neighbours(second, "x")
    back = move(normed, step_in)
    x_near, y_near, side, back = lax.optimization_barrier((x_near, y_near, side, back))
    x_far, y_far = opposite(*x_near, "x", core), opposite(*y_near, "y", core)
    edge = TOK - BLOCK
    far_side = move(lax.dynamic_slice_in_dim(side, jnp.where(core == 0, edge, 0), BLOCK, 0), step_out)
    far_back = move(lax.dynamic_slice_in_dim(back, jnp.where(core == 0, 0, edge), BLOCK, 0), step_in)
    back_other = swap(back)
    tokens_here = (normed, side, back, far_side, far_back)
    tokens_other = (normed_other, side_other, back_other, swap(far_side), swap(far_back))
    pieces = [first, *y_near, y_far, second, *x_near, x_far]
    gains = jnp.pad(jnp.stack([q_gain, k_gain]), ((0, 0), (0, LANES - HEAD)))

    def one(pack, place, tokens_of):
        blocks = lax.dynamic_slice_in_dim(img_blocks, pack, 1, 0)[0]
        widths = lax.dynamic_slice_in_dim(img_width, pack, 1, 0)[0]
        row, column, first_at, length = places(blocks, widths, shard)
        info = jnp.stack([xh * 2 + xl, y, first_at[3], length[3], first_at[4], length[4], place]).astype(jnp.int32)
        return attend(info, tokens_of, angles(row, column), gains, pieces)

    theirs = one(xh * 2 + 1 - core, 1 - core, tokens_other)
    received = swap(theirs)
    ours = one(xh * 2 + core, core, tokens_here)
    left = jnp.where(core == 0, ours, received)
    right = jnp.where(core == 0, received, ours)
    whole = jnp.concatenate(
        [left[:, :THREE], right[:, :THREE], left[:, THREE:], right[:, THREE:]], axis=1
    )
    return whole[None]


def solution(mesh):
    devices = mesh.devices.reshape([SIZES[a] for a in AXES])
    fine = Mesh(devices, AXES)
    return jax.shard_map(
        shards,
        mesh=fine,
        in_specs=(
            P(("xh", "c"), ("y", "xl", "z"), None),
            P(),
            P(None, ("y", "xl", "z"), ("xh", "c")),
            P(),
            P(),
            P(),
            P(),
        ),
        out_specs=P(("xh", "c"), ("y", "xl", "z"), None),
        check_vma=False,
    )
```

```python
import functools
import itertools

import jax
import jax.numpy as jnp
from jax import lax
from jax.experimental import pallas as pl
from jax.experimental.pallas import tpu as pltpu
from jax.sharding import Mesh
from jax.sharding import PartitionSpec as P

HEAD = 96
BLOCK = 128
EPS = 1e-06
LANES = 128
AXES = ("xh", "c", "y", "xl", "z")
SIZES = {"xh": 2, "c": 2, "y": 4, "xl": 2, "z": 8}
D = 2304
TOK = 256
REACH = 3 * BLOCK
WIN = TOK + 2 * REACH
STEP = 256
THREE = 288
OTHERS = (1, -1, 2)


def move(value, where):
    pairs = []
    for place in itertools.product(*[range(SIZES[a]) for a in AXES]):
        target = where(dict(zip(AXES, place)))
        if target is None:
            continue
        source_at = target_at = 0
        for axis, coordinate in zip(AXES, place):
            source_at = source_at * SIZES[axis] + coordinate
            target_at = target_at * SIZES[axis] + target[axis]
        pairs.append((source_at, target_at))
    return lax.ppermute(value, AXES, pairs)


def along(axis, by):
    def where(place):
        if axis == "x":
            x = (place["xh"] * 2 + place["xl"] + by) % 4
            return {**place, "xh": x // 2, "xl": x % 2}
        return {**place, axis: (place[axis] + by) % SIZES[axis]}

    return where


def along_seq(by):
    def where(place):
        s = (place["y"] * 2 + place["xl"]) * 8 + place["z"] + by
        if not 0 <= s < 64:
            return None
        return {**place, "y": s // 16, "xl": s // 8 % 2, "z": s % 8}

    return where


def mirrored(axis_move, by):
    def where(place):
        return axis_move(by if place["c"] == 0 else -by)(place)

    return where


def neighbours(value, axis):
    return move(value, along(axis, -1)), move(value, along(axis, 1))


def opposite(ahead, behind, axis, core):
    return move(jnp.where(core == 0, behind, ahead), mirrored(functools.partial(along, axis), 1))


def gather_z(mine):
    z = lax.axis_index("z")
    ahead, behind = move(mine, along("z", -1)), move(mine, along("z", 1))
    three = jnp.stack([behind, mine, ahead])
    far_ahead, far_behind = move(three, along("z", -3)), move(three, along("z", 3))
    relative = jnp.concatenate([far_behind, three, far_ahead[:2]], axis=0)
    doubled = jnp.concatenate([relative, relative], axis=0)
    return lax.dynamic_slice_in_dim(doubled, (12 - z) % 8, 8, 0)


def attend_kernel(info, table, gains, spread, *refs):
    tokens_of, pieces = refs[:5], refs[5:13]
    out, w_all, x_all, keys, values, w_sem, x_sem = refs[13:]
    x_here, y_here, flipped = info[0], info[1], info[6]
    left, right = BLOCK, REACH + TOK
    starts = (
        REACH,
        jnp.where(flipped == 0, left, right),
        jnp.where(flipped == 0, right, left),
        jnp.where(flipped == 0, 0, WIN - BLOCK),
        jnp.where(flipped == 0, WIN - BLOCK, 0),
    )
    for source, at in zip(tokens_of, starts):
        rows = pl.ds(pl.multiple_of(at, BLOCK), source.shape[0])
        pltpu.make_async_copy(source, x_all.at[rows], x_sem).start()

    def fetch(column_half):
        for half in range(2):
            for far in range(4):
                for near in range(4):
                    by_near, by_far = ((0,) + OTHERS)[near], ((0,) + OTHERS)[far]
                    dx, dy = (by_near, by_far) if half == 0 else (by_far, by_near)
                    x_from = lax.rem(x_here + (dx + 4), 4)
                    y_from = lax.rem(y_here + (dy + 4), 4)
                    row = (2 * y_from + lax.rem(x_from, 2)) * 288 + half * 144
                    rows = pl.ds(pl.multiple_of(row, 144), 144)

                    @pl.when(lax.div(x_from, 2) == column_half)
                    def _():
                        pltpu.make_async_copy(
                            pieces[4 * half + far].at[near], w_all.at[column_half, rows], w_sem.at[column_half]
                        ).start()

    fetch(0)
    fetch(1)
    pltpu.make_async_copy(x_all, x_all, x_sem).wait()
    low = lax.rem(lax.broadcasted_iota(jnp.int32, (1, LANES), 1), 48) < 24

    def unit(wide):
        square = wide * wide
        high = square.astype(jnp.bfloat16)
        rest = (square - high.astype(jnp.float32)).astype(jnp.bfloat16)
        total = jnp.dot(high, spread[...], preferred_element_type=jnp.float32)
        total = total + jnp.dot(rest, spread[...], preferred_element_type=jnp.float32)
        return lax.rsqrt(total * (1.0 / HEAD) + EPS)

    def turn(value, cosine, sine):
        partner = jnp.where(low, pltpu.roll(value, LANES - 24, 1), pltpu.roll(value, 24, 1))
        return value * cosine + partner * sine

    def heads(wide, gain, rows):
        scale = unit(wide[:, :384])
        cosine, sine = table[0, rows], table[1, rows]
        for head in range(3):
            part = wide[:, HEAD * head : HEAD * head + LANES] * scale[:, LANES * head : LANES * (head + 1)]
            yield turn(part * gain, cosine, sine).astype(jnp.bfloat16)

    mixed = []
    for column_half in range(2):
        pltpu.make_async_copy(
            w_all.at[column_half], w_all.at[column_half], w_sem.at[column_half]
        ).wait()
        for step in range(WIN // STEP):
            rows = pl.ds(step * STEP, STEP)
            raw = jnp.dot(
                x_all[rows], w_all[column_half, :, 0:640], preferred_element_type=jnp.float32
            )
            for head, turned in enumerate(heads(raw, gains[1:2], rows)):
                keys[3 * column_half + head, rows] = turned
            for head in range(3):
                part = raw[:, THREE + HEAD * head : THREE + HEAD * head + LANES]
                values[3 * column_half + head, rows] = part.astype(jnp.bfloat16)
        mine = pl.ds(REACH, TOK)
        raw = jnp.dot(
            x_all[mine], w_all[column_half, :, 512:864], preferred_element_type=jnp.float32
        )
        wide = jnp.concatenate([raw[:, 64:], jnp.zeros((TOK, 128), jnp.float32)], axis=1)
        queries = list(heads(wide, gains[0:1], mine))
        places_of = [(head, block) for head in range(3) for block in range(2)]
        scores, probs = [], []
        for head, block in places_of:
            window = pl.ds(pl.multiple_of(info[2 + 2 * block], BLOCK), 4 * BLOCK)
            scores.append(
                lax.dot_general(
                    queries[head][BLOCK * block : BLOCK * (block + 1)],
                    keys[3 * column_half + head, window],
                    (((1,), (1,)), ((), ())),
                    preferred_element_type=jnp.float32,
                )
            )
        column = lax.broadcasted_iota(jnp.int32, (1, 4 * BLOCK), 1)
        for (head, block), score in zip(places_of, scores):
            score = jnp.where(column < info[3 + 2 * block], score * (HEAD ** (-0.5)), -1e30)
            expo = jnp.exp(score - jnp.max(score, axis=1, keepdims=True))
            probs.append((expo * (1.0 / jnp.sum(expo, axis=1, keepdims=True))).astype(jnp.bfloat16))
        both = []
        for (head, block), prob in zip(places_of, probs):
            window = pl.ds(pl.multiple_of(info[2 + 2 * block], BLOCK), 4 * BLOCK)
            both.append(
                jnp.dot(prob, values[3 * column_half + head, window], preferred_element_type=jnp.float32)
            )
            if block == 1:
                mixed.append(jnp.concatenate(both, axis=0)[:, :HEAD])
                both = []
    out[...] = jnp.concatenate(mixed, axis=1).astype(jnp.bfloat16)


def attend(info, table, gains, spread, tokens_of, pieces):
    anywhere = pl.BlockSpec(memory_space=pl.ANY)
    vmem = pl.BlockSpec(memory_space=pltpu.VMEM)
    return pl.pallas_call(
        attend_kernel,
        out_shape=jax.ShapeDtypeStruct((TOK, 2 * THREE), jnp.bfloat16),
        in_specs=[pl.BlockSpec(memory_space=pltpu.SMEM), vmem, vmem, vmem] + [anywhere] * 13,
        out_specs=vmem,
        scratch_shapes=[
            pltpu.VMEM((2, D, 3 * THREE), jnp.bfloat16),
            pltpu.VMEM((WIN, D), jnp.bfloat16),
            pltpu.VMEM((6, WIN, LANES), jnp.bfloat16),
            pltpu.VMEM((6, WIN, LANES), jnp.bfloat16),
            pltpu.SemaphoreType.DMA((2,)),
            pltpu.SemaphoreType.DMA,
        ],
        compiler_params=pltpu.CompilerParams(vmem_limit_bytes=60 * 2**20),
        cost_estimate=pl.CostEstimate(
            flops=2 * D * 864 * 2 * 1024, bytes_accessed=14 * 2**20, transcendentals=2**20
        ),
    )(info, table, gains, spread, *tokens_of, *pieces)


def places(blocks, widths, shard):
    order = jnp.arange(64, dtype=jnp.int32)
    starts = jnp.sum(jnp.where(order[None, :] < order[:, None], blocks[None, :], 0), axis=1)
    block_at = shard * 2 - 3 + jnp.arange(8, dtype=jnp.int32)
    begun = starts[None, :] <= block_at[:, None]
    inside = begun & (block_at[:, None] < (starts + blocks)[None, :])
    begin = jnp.sum(jnp.where(inside, starts[None, :], 0), axis=1)
    length = jnp.sum(jnp.where(inside, blocks[None, :], 0), axis=1)
    across = jnp.maximum(jnp.sum(jnp.where(inside, widths[None, :], 0), axis=1), 1)
    offset = (block_at - begin)[:, None] * BLOCK + jnp.arange(BLOCK, dtype=jnp.int32)[None, :]
    row, column = lax.div(offset, across[:, None] + 0 * offset), lax.rem(offset, across[:, None] + 0 * offset)
    back = (begin - block_at + jnp.arange(8, dtype=jnp.int32)) * BLOCK
    return row.reshape(WIN), column.reshape(WIN), back, length * BLOCK


def angles(row, column):
    lane = jnp.arange(LANES, dtype=jnp.int32)
    freq = 10000.0 ** (-(lane % 24).astype(jnp.float32) / 24)
    place = jnp.where(lane[None, :] < 48, row[:, None], column[:, None]).astype(jnp.float32)
    angle = place * freq[None, :]
    sign = jnp.where(lane % 48 < 24, -1.0, 1.0)
    real = lane < HEAD
    return jnp.stack(
        [jnp.where(real, jnp.cos(angle), 0.0), jnp.where(real, jnp.sin(angle) * sign, 0.0)]
    )


def spread_heads():
    feature, lane = jnp.arange(384)[:, None], jnp.arange(384)[None, :]
    return ((feature // HEAD == lane // LANES) & (feature < THREE)).astype(jnp.bfloat16)


def shards(tokens, norm_gain, w_qkv, q_gain, k_gain, img_blocks, img_width):
    xh, core, y, xl, z = (lax.axis_index(a) for a in AXES)
    shard = (y * 2 + xl) * 8 + z
    mine = jnp.concatenate([w_qkv[1], w_qkv[2], w_qkv[0]], axis=1)
    rows = gather_z(mine).reshape(2, 144, 3 * THREE)
    wide = tokens[0].astype(jnp.float32)
    scaled = wide * lax.rsqrt(jnp.mean(wide * wide, axis=-1, keepdims=True) + EPS) * norm_gain
    normed = scaled.astype(jnp.bfloat16)
    swap = functools.partial(move, where=along("c", 1))
    step_out, step_in = mirrored(along_seq, 1), mirrored(along_seq, -1)
    normed_other = swap(normed)
    rows, normed = lax.optimization_barrier((rows, normed))
    gains = jnp.pad(jnp.stack([q_gain, k_gain]), ((0, 0), (0, LANES - HEAD)))

    def about(pack, place):
        blocks = lax.dynamic_slice_in_dim(img_blocks, pack, 1, 0)[0]
        widths = lax.dynamic_slice_in_dim(img_width, pack, 1, 0)[0]
        row, column, first_at, length = places(blocks, widths, shard)
        info = jnp.stack([xh * 2 + xl, y, first_at[3], length[3], first_at[4], length[4], place])
        return info.astype(jnp.int32), angles(row, column), gains, spread_heads()

    given = about(xh * 2 + 1 - core, 1 - core), about(xh * 2 + core, core)
    x_near, y_near = neighbours(rows[0], "x"), neighbours(rows[1], "y")
    side = move(normed, step_out)
    first = jnp.stack([rows[0], *x_near, opposite(*x_near, "x", core)])
    second = jnp.stack([rows[1], *y_near, opposite(*y_near, "y", core)])
    first, second, side, normed = lax.optimization_barrier((first, second, side, normed))
    side_other = swap(side)
    y_near, x_near = neighbours(first, "y"), neighbours(second, "x")
    back = move(normed, step_in)
    x_near, y_near, side, back, given = lax.optimization_barrier((x_near, y_near, side, back, given))
    x_far, y_far = opposite(*x_near, "x", core), opposite(*y_near, "y", core)
    edge = TOK - BLOCK
    far_side = move(lax.dynamic_slice_in_dim(side, jnp.where(core == 0, edge, 0), BLOCK, 0), step_out)
    far_back = move(lax.dynamic_slice_in_dim(back, jnp.where(core == 0, 0, edge), BLOCK, 0), step_in)
    back_other = swap(back)
    tokens_here = (normed, side, back, far_side, far_back)
    tokens_other = (normed_other, side_other, back_other, swap(far_side), swap(far_back))
    pieces = [first, *y_near, y_far, second, *x_near, x_far]
    theirs = attend(*given[0], tokens_other, pieces)
    received = swap(theirs)
    ours = attend(*given[1], tokens_here, pieces)
    left = jnp.where(core == 0, ours, received)
    right = jnp.where(core == 0, received, ours)
    whole = jnp.concatenate(
        [left[:, :THREE], right[:, :THREE], left[:, THREE:], right[:, THREE:]], axis=1
    )
    return whole[None]


def solution(mesh):
    devices = mesh.devices.reshape([SIZES[a] for a in AXES])
    fine = Mesh(devices, AXES)
    return jax.shard_map(
        shards,
        mesh=fine,
        in_specs=(
            P(("xh", "c"), ("y", "xl", "z"), None),
            P(),
            P(None, ("y", "xl", "z"), ("xh", "c")),
            P(),
            P(),
            P(),
            P(),
        ),
        out_specs=P(("xh", "c"), ("y", "xl", "z"), None),
        check_vma=False,
    )
```

```python
import functools
import itertools

import jax
import jax.numpy as jnp
from jax import lax
from jax.experimental import pallas as pl
from jax.experimental.pallas import tpu as pltpu
from jax.sharding import Mesh
from jax.sharding import PartitionSpec as P

HEAD = 96
BLOCK = 128
EPS = 1e-06
LANES = 128
AXES = ("xh", "c", "y", "xl", "z")
SIZES = {"xh": 2, "c": 2, "y": 4, "xl": 2, "z": 8}
D = 2304
TOK = 256
REACH = 3 * BLOCK
WIN = TOK + 2 * REACH
STEP = 256
THREE = 288
OTHERS = (1, -1, 2)


def move(value, where):
    pairs = []
    for place in itertools.product(*[range(SIZES[a]) for a in AXES]):
        target = where(dict(zip(AXES, place)))
        if target is None:
            continue
        source_at = target_at = 0
        for axis, coordinate in zip(AXES, place):
            source_at = source_at * SIZES[axis] + coordinate
            target_at = target_at * SIZES[axis] + target[axis]
        pairs.append((source_at, target_at))
    return lax.ppermute(value, AXES, pairs)


def along(axis, by):
    def where(place):
        if axis == "x":
            x = (place["xh"] * 2 + place["xl"] + by) % 4
            return {**place, "xh": x // 2, "xl": x % 2}
        return {**place, axis: (place[axis] + by) % SIZES[axis]}

    return where


def along_seq(by):
    def where(place):
        s = (place["y"] * 2 + place["xl"]) * 8 + place["z"] + by
        if not 0 <= s < 64:
            return None
        return {**place, "y": s // 16, "xl": s // 8 % 2, "z": s % 8}

    return where


def mirrored(axis_move, by):
    def where(place):
        return axis_move(by if place["c"] == 0 else -by)(place)

    return where


def neighbours(value, axis):
    return move(value, along(axis, -1)), move(value, along(axis, 1))


def ring(value, axis):
    return [value] + [move(value, along(axis, -by)) for by in OTHERS]


def opposite(ahead, behind, axis, core):
    return move(jnp.where(core == 0, behind, ahead), mirrored(functools.partial(along, axis), 1))


def gather_z(mine):
    z = lax.axis_index("z")
    ahead, behind = move(mine, along("z", -1)), move(mine, along("z", 1))
    three = jnp.stack([behind, mine, ahead])
    far_ahead, far_behind = move(three, along("z", -3)), move(three, along("z", 3))
    relative = jnp.concatenate([far_behind, three, far_ahead[:2]], axis=0)
    doubled = jnp.concatenate([relative, relative], axis=0)
    return lax.dynamic_slice_in_dim(doubled, (12 - z) % 8, 8, 0)


def attend_kernel(info, table, gains, spread, *refs):
    tokens_of, pieces = refs[:5], refs[5:13]
    out, w_all, x_all, keys, values, w_sem, x_sem = refs[13:]
    x_here, y_here, flipped = info[0], info[1], info[2]
    left, right = BLOCK, REACH + TOK
    starts = (
        REACH,
        jnp.where(flipped == 0, left, right),
        jnp.where(flipped == 0, right, left),
        jnp.where(flipped == 0, 0, WIN - BLOCK),
        jnp.where(flipped == 0, WIN - BLOCK, 0),
    )
    for source, at in zip(tokens_of, starts):
        rows = pl.ds(pl.multiple_of(at, BLOCK), source.shape[0])
        pltpu.make_async_copy(source, x_all.at[rows], x_sem).start()

    def fetch(column_half):
        for half in range(2):
            for far in range(4):
                for near in range(4):
                    by_near, by_far = ((0,) + OTHERS)[near], ((0,) + OTHERS)[far]
                    dx, dy = (by_near, by_far) if half == 0 else (by_far, by_near)
                    x_from = lax.rem(x_here + (dx + 4), 4)
                    y_from = lax.rem(y_here + (dy + 4), 4)
                    row = (2 * y_from + lax.rem(x_from, 2)) * 288 + half * 144
                    rows = pl.ds(pl.multiple_of(row, 144), 144)

                    @pl.when(lax.div(x_from, 2) == column_half)
                    def _():
                        pltpu.make_async_copy(
                            pieces[4 * half + far].at[near], w_all.at[column_half, rows], w_sem.at[column_half]
                        ).start()

    fetch(0)
    fetch(1)
    pltpu.make_async_copy(x_all, x_all, x_sem).wait()
    low = lax.rem(lax.broadcasted_iota(jnp.int32, (1, LANES), 1), 48) < 24

    def unit(wide):
        square = wide * wide
        high = square.astype(jnp.bfloat16)
        rest = (square - high.astype(jnp.float32)).astype(jnp.bfloat16)
        total = jnp.dot(high, spread[...], preferred_element_type=jnp.float32)
        total = total + jnp.dot(rest, spread[...], preferred_element_type=jnp.float32)
        return lax.rsqrt(total * (1.0 / HEAD) + EPS)

    def turn(value, cosine, sine):
        partner = jnp.where(low, pltpu.roll(value, LANES - 24, 1), pltpu.roll(value, 24, 1))
        return value * cosine + partner * sine

    def heads(wide, gain, rows):
        scale = unit(wide[:, :384])
        cosine, sine = table[0, rows], table[1, rows]
        for head in range(3):
            part = wide[:, HEAD * head : HEAD * head + LANES] * scale[:, LANES * head : LANES * (head + 1)]
            yield turn(part * gain, cosine, sine).astype(jnp.bfloat16)

    mixed = []
    for column_half in range(2):
        pltpu.make_async_copy(
            w_all.at[column_half], w_all.at[column_half], w_sem.at[column_half]
        ).wait()
        for step in range(WIN // STEP):
            rows = pl.ds(step * STEP, STEP)
            raw = jnp.dot(
                x_all[rows], w_all[column_half, :, 0:640], preferred_element_type=jnp.float32
            )
            for head, turned in enumerate(heads(raw, gains[1:2], rows)):
                keys[3 * column_half + head, rows] = turned
            for head in range(3):
                part = raw[:, THREE + HEAD * head : THREE + HEAD * head + LANES]
                values[3 * column_half + head, rows] = part.astype(jnp.bfloat16)
        mine = pl.ds(REACH, TOK)
        raw = jnp.dot(
            x_all[mine], w_all[column_half, :, 512:864], preferred_element_type=jnp.float32
        )
        wide = jnp.concatenate([raw[:, 64:], jnp.zeros((TOK, 128), jnp.float32)], axis=1)
        queries = list(heads(wide, gains[0:1], mine))
        places_of = [(head, block) for head in range(3) for block in range(2)]
        scores, probs = [], []
        for head, block in places_of:
            window = pl.ds(pl.multiple_of(info[3 + block], BLOCK), 4 * BLOCK)
            scores.append(
                lax.dot_general(
                    queries[head][BLOCK * block : BLOCK * (block + 1)],
                    keys[3 * column_half + head, window],
                    (((1,), (1,)), ((), ())),
                    preferred_element_type=jnp.float32,
                )
            )
        column = lax.broadcasted_iota(jnp.int32, (1, 4 * BLOCK), 1)
        for (head, block), score in zip(places_of, scores):
            score = jnp.where(column < info[5 + block], score * (HEAD ** (-0.5)), -1e30)
            expo = jnp.exp(score - jnp.max(score, axis=1, keepdims=True))
            probs.append((expo * (1.0 / jnp.sum(expo, axis=1, keepdims=True))).astype(jnp.bfloat16))
        both = []
        for (head, block), prob in zip(places_of, probs):
            window = pl.ds(pl.multiple_of(info[3 + block], BLOCK), 4 * BLOCK)
            both.append(
                jnp.dot(prob, values[3 * column_half + head, window], preferred_element_type=jnp.float32)
            )
            if block == 1:
                mixed.append(jnp.concatenate(both, axis=0)[:, :HEAD])
                both = []
    out[...] = jnp.concatenate(mixed, axis=1).astype(jnp.bfloat16)


def attend(info, table, gains, spread, tokens_of, pieces):
    anywhere = pl.BlockSpec(memory_space=pl.ANY)
    vmem = pl.BlockSpec(memory_space=pltpu.VMEM)
    return pl.pallas_call(
        attend_kernel,
        out_shape=jax.ShapeDtypeStruct((TOK, 2 * THREE), jnp.bfloat16),
        in_specs=[pl.BlockSpec(memory_space=pltpu.SMEM), vmem, vmem, vmem] + [anywhere] * 13,
        out_specs=vmem,
        scratch_shapes=[
            pltpu.VMEM((2, D, 3 * THREE), jnp.bfloat16),
            pltpu.VMEM((WIN, D), jnp.bfloat16),
            pltpu.VMEM((6, WIN, LANES), jnp.bfloat16),
            pltpu.VMEM((6, WIN, LANES), jnp.bfloat16),
            pltpu.SemaphoreType.DMA((2,)),
            pltpu.SemaphoreType.DMA,
        ],
        compiler_params=pltpu.CompilerParams(vmem_limit_bytes=60 * 2**20),
        cost_estimate=pl.CostEstimate(
            flops=2 * D * 864 * 2 * 1024, bytes_accessed=14 * 2**20, transcendentals=2**20
        ),
    )(info, table, gains, spread, *tokens_of, *pieces)


def places(img_blocks, img_width, pack, shard):
    blocks = lax.dynamic_slice_in_dim(img_blocks, pack, 1, 0)[0]
    widths = lax.dynamic_slice_in_dim(img_width, pack, 1, 0)[0]
    order = jnp.arange(64, dtype=jnp.int32)
    starts = jnp.sum(jnp.where(order[None, :] < order[:, None], blocks[None, :], 0), axis=1)
    block_at = shard * 2 - 3 + jnp.arange(8, dtype=jnp.int32)
    begun = starts[None, :] <= block_at[:, None]
    inside = begun & (block_at[:, None] < (starts + blocks)[None, :])
    begin = jnp.sum(jnp.where(inside, starts[None, :], 0), axis=1)
    length = jnp.sum(jnp.where(inside, blocks[None, :], 0), axis=1)
    across = jnp.maximum(jnp.sum(jnp.where(inside, widths[None, :], 0), axis=1), 1)
    offset = (block_at - begin)[:, None] * BLOCK + jnp.arange(BLOCK, dtype=jnp.int32)[None, :]
    row, column = lax.div(offset, across[:, None] + 0 * offset), lax.rem(offset, across[:, None] + 0 * offset)
    back = (begin - block_at + jnp.arange(8, dtype=jnp.int32)) * BLOCK
    return row.reshape(WIN), column.reshape(WIN), back, length * BLOCK


def angles(row, column):
    lane = jnp.arange(LANES, dtype=jnp.int32)
    freq = 10000.0 ** (-(lane % 24).astype(jnp.float32) / 24)
    place = jnp.where(lane[None, :] < 48, row[:, None], column[:, None]).astype(jnp.float32)
    angle = place * freq[None, :]
    sign = jnp.where(lane % 48 < 24, -1.0, 1.0)
    real = lane < HEAD
    return jnp.stack(
        [jnp.where(real, jnp.cos(angle), 0.0), jnp.where(real, jnp.sin(angle) * sign, 0.0)]
    )


def spread_heads():
    feature, lane = jnp.arange(384)[:, None], jnp.arange(384)[None, :]
    return ((feature // HEAD == lane // LANES) & (feature < THREE)).astype(jnp.bfloat16)


def shards(tokens, norm_gain, w_qkv, q_gain, k_gain, img_blocks, img_width):
    xh, core, y, xl, z = (lax.axis_index(a) for a in AXES)
    shard = (y * 2 + xl) * 8 + z
    mine = jnp.concatenate([w_qkv[1], w_qkv[2], w_qkv[0]], axis=1)
    rows = gather_z(mine).reshape(2, 144, 3 * THREE)
    wide = tokens[0].astype(jnp.float32)
    scaled = wide * lax.rsqrt(jnp.mean(wide * wide, axis=-1, keepdims=True) + EPS) * norm_gain
    normed = scaled.astype(jnp.bfloat16)
    swap = functools.partial(move, where=along("c", 1))
    step_out, step_in = mirrored(along_seq, 1), mirrored(along_seq, -1)
    normed_other = swap(normed)
    gains = jnp.pad(jnp.stack([q_gain, k_gain]), ((0, 0), (0, LANES - HEAD)))
    mine_at = [places(img_blocks, img_width, pack, shard) for pack in (xh * 2 + 1 - core, xh * 2 + core)]
    side = move(normed, step_out)
    rows, side, normed_other, mine_at = lax.optimization_barrier((rows, side, normed_other, mine_at))
    first = jnp.stack(ring(rows[0], "x"))
    second = jnp.stack(ring(rows[1], "y"))
    side_other = swap(side)
    first, second, side_other, normed = lax.optimization_barrier((first, second, side_other, normed))
    y_near, x_near = neighbours(first, "y"), neighbours(second, "x")
    back = move(normed, step_in)
    tables = [angles(row, column) for row, column, _, _ in mine_at]
    x_near, y_near, side, back, tables = lax.optimization_barrier((x_near, y_near, side, back, tables))
    x_far, y_far = opposite(*x_near, "x", core), opposite(*y_near, "y", core)
    edge = TOK - BLOCK
    far_side = move(lax.dynamic_slice_in_dim(side, jnp.where(core == 0, edge, 0), BLOCK, 0), step_out)
    far_back = move(lax.dynamic_slice_in_dim(back, jnp.where(core == 0, 0, edge), BLOCK, 0), step_in)
    back_other = swap(back)
    tokens_here = (normed, side, back, far_side, far_back)
    tokens_other = (normed_other, side_other, back_other, swap(far_side), swap(far_back))

    def info(which, place):
        _, _, first_at, length = mine_at[which]
        scalars = jnp.stack([xh * 2 + xl, y, place]).astype(jnp.int32)
        return jnp.concatenate([scalars, first_at[3:5], length[3:5]])

    pieces = [first, *y_near, y_far, second, *x_near, x_far]
    theirs = attend(info(0, 1 - core), tables[0], gains, spread_heads(), tokens_other, pieces)
    received = swap(theirs)
    ours = attend(info(1, core), tables[1], gains, spread_heads(), tokens_here, pieces)
    left = jnp.where(core == 0, ours, received)
    right = jnp.where(core == 0, received, ours)
    whole = jnp.concatenate(
        [left[:, :THREE], right[:, :THREE], left[:, THREE:], right[:, THREE:]], axis=1
    )
    return whole[None]


def solution(mesh):
    devices = mesh.devices.reshape([SIZES[a] for a in AXES])
    fine = Mesh(devices, AXES)
    return jax.shard_map(
        shards,
        mesh=fine,
        in_specs=(
            P(("xh", "c"), ("y", "xl", "z"), None),
            P(),
            P(None, ("y", "xl", "z"), ("xh", "c")),
            P(),
            P(),
            P(),
            P(),
        ),
        out_specs=P(("xh", "c"), ("y", "xl", "z"), None),
        check_vma=False,
    )
```

```python
import functools
import itertools

import jax
import jax.numpy as jnp
from jax import lax
from jax.experimental import pallas as pl
from jax.experimental.pallas import tpu as pltpu
from jax.sharding import Mesh
from jax.sharding import PartitionSpec as P

HEAD = 96
BLOCK = 128
EPS = 1e-06
LANES = 128
AXES = ("xh", "c", "y", "xl", "z")
SIZES = {"xh": 2, "c": 2, "y": 4, "xl": 2, "z": 8}
D = 2304
TOK = 256
REACH = 3 * BLOCK
WIN = TOK + 2 * REACH
STEP = 256
THREE = 288
OTHERS = (1, -1, 2)


def move(value, where):
    pairs = []
    for place in itertools.product(*[range(SIZES[a]) for a in AXES]):
        target = where(dict(zip(AXES, place)))
        if target is None:
            continue
        source_at = target_at = 0
        for axis, coordinate in zip(AXES, place):
            source_at = source_at * SIZES[axis] + coordinate
            target_at = target_at * SIZES[axis] + target[axis]
        pairs.append((source_at, target_at))
    return lax.ppermute(value, AXES, pairs)


def along(axis, by):
    def where(place):
        if axis == "x":
            x = (place["xh"] * 2 + place["xl"] + by) % 4
            return {**place, "xh": x // 2, "xl": x % 2}
        return {**place, axis: (place[axis] + by) % SIZES[axis]}

    return where


def along_seq(by):
    def where(place):
        s = (place["y"] * 2 + place["xl"]) * 8 + place["z"] + by
        if not 0 <= s < 64:
            return None
        return {**place, "y": s // 16, "xl": s // 8 % 2, "z": s % 8}

    return where


def mirrored(axis_move, by):
    def where(place):
        return axis_move(by if place["c"] == 0 else -by)(place)

    return where


def neighbours(value, axis):
    return move(value, along(axis, -1)), move(value, along(axis, 1))


def opposite(ahead, behind, axis, core):
    return move(jnp.where(core == 0, behind, ahead), mirrored(functools.partial(along, axis), 1))


def gather_z(mine):
    z = lax.axis_index("z")
    ahead, behind = move(mine, along("z", -1)), move(mine, along("z", 1))
    three = jnp.stack([behind, mine, ahead])
    far_ahead, far_behind = move(three, along("z", -3)), move(three, along("z", 3))
    relative = jnp.concatenate([far_behind, three, far_ahead[:2]], axis=0)
    doubled = jnp.concatenate([relative, relative], axis=0)
    return lax.dynamic_slice_in_dim(doubled, (12 - z) % 8, 8, 0)


def attend_kernel(info, table, gains, spread, *refs):
    tokens_of, pieces = refs[:5], refs[5:13]
    out, w_all, x_all, keys, values, w_sem, x_sem = refs[13:]
    x_here, y_here, flipped = info[0], info[1], info[2]
    left, right = BLOCK, REACH + TOK
    starts = (
        REACH,
        jnp.where(flipped == 0, left, right),
        jnp.where(flipped == 0, right, left),
        jnp.where(flipped == 0, 0, WIN - BLOCK),
        jnp.where(flipped == 0, WIN - BLOCK, 0),
    )
    for source, at in zip(tokens_of, starts):
        rows = pl.ds(pl.multiple_of(at, BLOCK), source.shape[0])
        pltpu.make_async_copy(source, x_all.at[rows], x_sem).start()

    def fetch(column_half):
        for half in range(2):
            for far in range(4):
                for near in range(4):
                    by_near, by_far = ((0,) + OTHERS)[near], ((0,) + OTHERS)[far]
                    dx, dy = (by_near, by_far) if half == 0 else (by_far, by_near)
                    x_from = lax.rem(x_here + (dx + 4), 4)
                    y_from = lax.rem(y_here + (dy + 4), 4)
                    row = (2 * y_from + lax.rem(x_from, 2)) * 288 + half * 144
                    rows = pl.ds(pl.multiple_of(row, 144), 144)

                    @pl.when(lax.div(x_from, 2) == column_half)
                    def _():
                        pltpu.make_async_copy(
                            pieces[4 * half + far].at[near], w_all.at[column_half, rows], w_sem.at[column_half]
                        ).start()

    fetch(0)
    fetch(1)
    pltpu.make_async_copy(x_all, x_all, x_sem).wait()
    low = lax.rem(lax.broadcasted_iota(jnp.int32, (1, LANES), 1), 48) < 24

    def unit(wide):
        square = wide * wide
        high = square.astype(jnp.bfloat16)
        rest = (square - high.astype(jnp.float32)).astype(jnp.bfloat16)
        total = jnp.dot(high, spread[...], preferred_element_type=jnp.float32)
        total = total + jnp.dot(rest, spread[...], preferred_element_type=jnp.float32)
        return lax.rsqrt(total * (1.0 / HEAD) + EPS)

    def turn(value, cosine, sine):
        partner = jnp.where(low, pltpu.roll(value, LANES - 24, 1), pltpu.roll(value, 24, 1))
        return value * cosine + partner * sine

    def heads(wide, gain, rows):
        scale = unit(wide[:, :384])
        cosine, sine = table[0, rows], table[1, rows]
        for head in range(3):
            part = wide[:, HEAD * head : HEAD * head + LANES] * scale[:, LANES * head : LANES * (head + 1)]
            yield turn(part * gain, cosine, sine).astype(jnp.bfloat16)

    mixed = []
    for column_half in range(2):
        pltpu.make_async_copy(
            w_all.at[column_half], w_all.at[column_half], w_sem.at[column_half]
        ).wait()
        for step in range(WIN // STEP):
            rows = pl.ds(step * STEP, STEP)
            raw = jnp.dot(
                x_all[rows], w_all[column_half, :, 0:640], preferred_element_type=jnp.float32
            )
            for head, turned in enumerate(heads(raw, gains[1:2], rows)):
                keys[3 * column_half + head, rows] = turned
            for head in range(3):
                part = raw[:, THREE + HEAD * head : THREE + HEAD * head + LANES]
                values[3 * column_half + head, rows] = part.astype(jnp.bfloat16)
        mine = pl.ds(REACH, TOK)
        raw = jnp.dot(
            x_all[mine], w_all[column_half, :, 512:864], preferred_element_type=jnp.float32
        )
        wide = jnp.concatenate([raw[:, 64:], jnp.zeros((TOK, 128), jnp.float32)], axis=1)
        queries = list(heads(wide, gains[0:1], mine))
        places_of = [(head, block) for head in range(3) for block in range(2)]
        scores, probs = [], []
        for head, block in places_of:
            window = pl.ds(pl.multiple_of(info[3 + block], BLOCK), 4 * BLOCK)
            scores.append(
                lax.dot_general(
                    queries[head][BLOCK * block : BLOCK * (block + 1)],
                    keys[3 * column_half + head, window],
                    (((1,), (1,)), ((), ())),
                    preferred_element_type=jnp.float32,
                )
            )
        column = lax.broadcasted_iota(jnp.int32, (1, 4 * BLOCK), 1)
        for (head, block), score in zip(places_of, scores):
            score = jnp.where(column < info[5 + block], score * (HEAD ** (-0.5)), -1e30)
            expo = jnp.exp(score - jnp.max(score, axis=1, keepdims=True))
            probs.append((expo * (1.0 / jnp.sum(expo, axis=1, keepdims=True))).astype(jnp.bfloat16))
        both = []
        for (head, block), prob in zip(places_of, probs):
            window = pl.ds(pl.multiple_of(info[3 + block], BLOCK), 4 * BLOCK)
            both.append(
                jnp.dot(prob, values[3 * column_half + head, window], preferred_element_type=jnp.float32)
            )
            if block == 1:
                mixed.append(jnp.concatenate(both, axis=0)[:, :HEAD])
                both = []
    out[...] = jnp.concatenate(mixed, axis=1).astype(jnp.bfloat16)


def attend(info, table, gains, spread, tokens_of, pieces):
    anywhere = pl.BlockSpec(memory_space=pl.ANY)
    vmem = pl.BlockSpec(memory_space=pltpu.VMEM)
    return pl.pallas_call(
        attend_kernel,
        out_shape=jax.ShapeDtypeStruct((TOK, 2 * THREE), jnp.bfloat16),
        in_specs=[pl.BlockSpec(memory_space=pltpu.SMEM), vmem, vmem, vmem] + [anywhere] * 13,
        out_specs=vmem,
        scratch_shapes=[
            pltpu.VMEM((2, D, 3 * THREE), jnp.bfloat16),
            pltpu.VMEM((WIN, D), jnp.bfloat16),
            pltpu.VMEM((6, WIN, LANES), jnp.bfloat16),
            pltpu.VMEM((6, WIN, LANES), jnp.bfloat16),
            pltpu.SemaphoreType.DMA((2,)),
            pltpu.SemaphoreType.DMA,
        ],
        compiler_params=pltpu.CompilerParams(vmem_limit_bytes=60 * 2**20),
        cost_estimate=pl.CostEstimate(
            flops=2 * D * 864 * 2 * 1024, bytes_accessed=14 * 2**20, transcendentals=2**20
        ),
    )(info, table, gains, spread, *tokens_of, *pieces)


def places(img_blocks, img_width, pack, shard):
    blocks = lax.dynamic_slice_in_dim(img_blocks, pack, 1, 0)[0]
    widths = lax.dynamic_slice_in_dim(img_width, pack, 1, 0)[0]
    order = jnp.arange(64, dtype=jnp.int32)
    starts = jnp.sum(jnp.where(order[None, :] < order[:, None], blocks[None, :], 0), axis=1)
    block_at = shard * 2 - 3 + jnp.arange(8, dtype=jnp.int32)
    begun = starts[None, :] <= block_at[:, None]
    inside = begun & (block_at[:, None] < (starts + blocks)[None, :])
    begin = jnp.sum(jnp.where(inside, starts[None, :], 0), axis=1)
    length = jnp.sum(jnp.where(inside, blocks[None, :], 0), axis=1)
    across = jnp.maximum(jnp.sum(jnp.where(inside, widths[None, :], 0), axis=1), 1)
    offset = (block_at - begin)[:, None] * BLOCK + jnp.arange(BLOCK, dtype=jnp.int32)[None, :]
    row, column = lax.div(offset, across[:, None] + 0 * offset), lax.rem(offset, across[:, None] + 0 * offset)
    back = (begin - block_at + jnp.arange(8, dtype=jnp.int32)) * BLOCK
    return row.reshape(WIN), column.reshape(WIN), back, length * BLOCK


def angles(row, column):
    lane = jnp.arange(LANES, dtype=jnp.int32)
    freq = 10000.0 ** (-(lane % 24).astype(jnp.float32) / 24)
    place = jnp.where(lane[None, :] < 48, row[:, None], column[:, None]).astype(jnp.float32)
    angle = place * freq[None, :]
    sign = jnp.where(lane % 48 < 24, -1.0, 1.0)
    real = lane < HEAD
    return jnp.stack(
        [jnp.where(real, jnp.cos(angle), 0.0), jnp.where(real, jnp.sin(angle) * sign, 0.0)]
    )


def spread_heads():
    feature, lane = jnp.arange(384)[:, None], jnp.arange(384)[None, :]
    return ((feature // HEAD == lane // LANES) & (feature < THREE)).astype(jnp.bfloat16)


def shards(tokens, norm_gain, w_qkv, q_gain, k_gain, img_blocks, img_width):
    xh, core, y, xl, z = (lax.axis_index(a) for a in AXES)
    shard = (y * 2 + xl) * 8 + z
    mine = jnp.concatenate([w_qkv[1], w_qkv[2], w_qkv[0]], axis=1)
    rows = gather_z(mine).reshape(2, 144, 3 * THREE)
    wide = tokens[0].astype(jnp.float32)
    scaled = wide * lax.rsqrt(jnp.mean(wide * wide, axis=-1, keepdims=True) + EPS) * norm_gain
    normed = scaled.astype(jnp.bfloat16)
    swap = functools.partial(move, where=along("c", 1))
    step_out, step_in = mirrored(along_seq, 1), mirrored(along_seq, -1)
    normed_other = swap(normed)
    gains = jnp.pad(jnp.stack([q_gain, k_gain]), ((0, 0), (0, LANES - HEAD)))
    mine_at = [places(img_blocks, img_width, pack, shard) for pack in (xh * 2 + 1 - core, xh * 2 + core)]
    rows, normed, normed_other, mine_at = lax.optimization_barrier((rows, normed, normed_other, mine_at))
    x_near, y_near = neighbours(rows[0], "x"), neighbours(rows[1], "y")
    side = move(normed, step_out)
    first = jnp.stack([rows[0], *x_near, opposite(*x_near, "x", core)])
    second = jnp.stack([rows[1], *y_near, opposite(*y_near, "y", core)])
    first, second, side, normed = lax.optimization_barrier((first, second, side, normed))
    y_near, x_near = neighbours(first, "y"), neighbours(second, "x")
    back = move(normed, step_in)
    side_other = swap(side)
    tables = [angles(row, column) for row, column, _, _ in mine_at]
    x_near, y_near, tables = lax.optimization_barrier((x_near, y_near, tables))
    x_far, y_far = opposite(*x_near, "x", core), opposite(*y_near, "y", core)
    x_near, y_near, side, back, side_other = lax.optimization_barrier((x_near, y_near, side, back, side_other))
    edge = TOK - BLOCK
    far_side = move(lax.dynamic_slice_in_dim(side, jnp.where(core == 0, edge, 0), BLOCK, 0), step_out)
    far_back = move(lax.dynamic_slice_in_dim(back, jnp.where(core == 0, 0, edge), BLOCK, 0), step_in)
    back_other = swap(back)
    tokens_here = (normed, side, back, far_side, far_back)
    far_other = swap(far_side), swap(far_back)

    def info(which, place):
        _, _, first_at, length = mine_at[which]
        scalars = jnp.stack([xh * 2 + xl, y, place]).astype(jnp.int32)
        return jnp.concatenate([scalars, first_at[3:5], length[3:5]])

    pieces = [first, *y_near, y_far, second, *x_near, x_far]
    ours = attend(info(1, core), tables[1], gains, spread_heads(), tokens_here, pieces)
    ours, far_other, back_other = lax.optimization_barrier((ours, far_other, back_other))
    tokens_other = (normed_other, side_other, back_other, *far_other)
    theirs = attend(info(0, 1 - core), tables[0], gains, spread_heads(), tokens_other, pieces)
    received = swap(theirs)
    left = jnp.where(core == 0, ours, received)
    right = jnp.where(core == 0, received, ours)
    whole = jnp.concatenate(
        [left[:, :THREE], right[:, :THREE], left[:, THREE:], right[:, THREE:]], axis=1
    )
    return whole[None]


def solution(mesh):
    devices = mesh.devices.reshape([SIZES[a] for a in AXES])
    fine = Mesh(devices, AXES)
    return jax.shard_map(
        shards,
        mesh=fine,
        in_specs=(
            P(("xh", "c"), ("y", "xl", "z"), None),
            P(),
            P(None, ("y", "xl", "z"), ("xh", "c")),
            P(),
            P(),
            P(),
            P(),
        ),
        out_specs=P(("xh", "c"), ("y", "xl", "z"), None),
        check_vma=False,
    )
```

```python
import functools
import itertools

import jax
import jax.numpy as jnp
from jax import lax
from jax.experimental import pallas as pl
from jax.experimental.pallas import tpu as pltpu
from jax.sharding import Mesh
from jax.sharding import PartitionSpec as P

HEAD = 96
BLOCK = 128
EPS = 1e-06
LANES = 128
AXES = ("xh", "c", "y", "xl", "z")
SIZES = {"xh": 2, "c": 2, "y": 4, "xl": 2, "z": 8}
D = 2304
TOK = 256
REACH = 3 * BLOCK
WIN = TOK + 2 * REACH
STEP = 256
THREE = 288
OTHERS = (1, -1, 2)


def move(value, where):
    pairs = []
    for place in itertools.product(*[range(SIZES[a]) for a in AXES]):
        target = where(dict(zip(AXES, place)))
        if target is None:
            continue
        source_at = target_at = 0
        for axis, coordinate in zip(AXES, place):
            source_at = source_at * SIZES[axis] + coordinate
            target_at = target_at * SIZES[axis] + target[axis]
        pairs.append((source_at, target_at))
    return lax.ppermute(value, AXES, pairs)


def along(axis, by):
    def where(place):
        if axis == "x":
            x = (place["xh"] * 2 + place["xl"] + by) % 4
            return {**place, "xh": x // 2, "xl": x % 2}
        return {**place, axis: (place[axis] + by) % SIZES[axis]}

    return where


def along_seq(by):
    def where(place):
        s = (place["y"] * 2 + place["xl"]) * 8 + place["z"] + by
        if not 0 <= s < 64:
            return None
        return {**place, "y": s // 16, "xl": s // 8 % 2, "z": s % 8}

    return where


def across_ends(place):
    if place["z"] not in (0, 7):
        return None
    target = along_seq(1 if place["z"] == 7 else -1)(place)
    return target and {**target, "z": place["z"]}


def mirrored(axis_move, by):
    def where(place):
        return axis_move(by if place["c"] == 0 else -by)(place)

    return where


def neighbours(value, axis):
    return move(value, along(axis, -1)), move(value, along(axis, 1))


def opposite(ahead, behind, axis, core):
    return move(jnp.where(core == 0, behind, ahead), mirrored(functools.partial(along, axis), 1))


def gather_z(mine):
    z = lax.axis_index("z")
    ahead, behind = move(mine, along("z", -1)), move(mine, along("z", 1))
    three = jnp.stack([behind, mine, ahead])
    far_ahead, far_behind = move(three, along("z", -3)), move(three, along("z", 3))
    relative = jnp.concatenate([far_behind, three, far_ahead[:2]], axis=0)
    doubled = jnp.concatenate([relative, relative], axis=0)
    return lax.dynamic_slice_in_dim(doubled, (12 - z) % 8, 8, 0)


def attend_kernel(info, table, gains, spread, *refs):
    tokens_of, pieces = refs[:5], refs[5:13]
    out, w_all, x_all, keys, values, w_sem, x_sem = refs[13:]
    x_here, y_here, flipped = info[0], info[1], info[2]
    left, right = BLOCK, REACH + TOK
    starts = (
        REACH,
        jnp.where(flipped == 0, left, right),
        jnp.where(flipped == 0, right, left),
        jnp.where(flipped == 0, 0, WIN - BLOCK),
        jnp.where(flipped == 0, WIN - BLOCK, 0),
    )
    for source, at in zip(tokens_of, starts):
        rows = pl.ds(pl.multiple_of(at, BLOCK), source.shape[0])
        pltpu.make_async_copy(source, x_all.at[rows], x_sem).start()

    def fetch(column_half):
        for half in range(2):
            for far in range(4):
                for near in range(4):
                    by_near, by_far = ((0,) + OTHERS)[near], ((0,) + OTHERS)[far]
                    dx, dy = (by_near, by_far) if half == 0 else (by_far, by_near)
                    x_from = lax.rem(x_here + (dx + 4), 4)
                    y_from = lax.rem(y_here + (dy + 4), 4)
                    row = (2 * y_from + lax.rem(x_from, 2)) * 288 + half * 144
                    rows = pl.ds(pl.multiple_of(row, 144), 144)

                    @pl.when(lax.div(x_from, 2) == column_half)
                    def _():
                        pltpu.make_async_copy(
                            pieces[4 * half + far].at[near], w_all.at[column_half, rows], w_sem.at[column_half]
                        ).start()

    fetch(0)
    fetch(1)
    pltpu.make_async_copy(x_all, x_all, x_sem).wait()
    low = lax.rem(lax.broadcasted_iota(jnp.int32, (1, LANES), 1), 48) < 24

    def unit(wide):
        square = wide * wide
        high = square.astype(jnp.bfloat16)
        rest = (square - high.astype(jnp.float32)).astype(jnp.bfloat16)
        total = jnp.dot(high, spread[...], preferred_element_type=jnp.float32)
        total = total + jnp.dot(rest, spread[...], preferred_element_type=jnp.float32)
        return lax.rsqrt(total * (1.0 / HEAD) + EPS)

    def turn(value, cosine, sine):
        partner = jnp.where(low, pltpu.roll(value, LANES - 24, 1), pltpu.roll(value, 24, 1))
        return value * cosine + partner * sine

    def heads(wide, gain, rows):
        scale = unit(wide[:, :384])
        cosine, sine = table[0, rows], table[1, rows]
        for head in range(3):
            part = wide[:, HEAD * head : HEAD * head + LANES] * scale[:, LANES * head : LANES * (head + 1)]
            yield turn(part * gain, cosine, sine).astype(jnp.bfloat16)

    mixed = []
    for column_half in range(2):
        pltpu.make_async_copy(
            w_all.at[column_half], w_all.at[column_half], w_sem.at[column_half]
        ).wait()
        for step in range(WIN // STEP):
            rows = pl.ds(step * STEP, STEP)
            raw = jnp.dot(
                x_all[rows], w_all[column_half, :, 0:640], preferred_element_type=jnp.float32
            )
            for head, turned in enumerate(heads(raw, gains[1:2], rows)):
                keys[3 * column_half + head, rows] = turned
            for head in range(3):
                part = raw[:, THREE + HEAD * head : THREE + HEAD * head + LANES]
                values[3 * column_half + head, rows] = part.astype(jnp.bfloat16)
        mine = pl.ds(REACH, TOK)
        raw = jnp.dot(
            x_all[mine], w_all[column_half, :, 512:864], preferred_element_type=jnp.float32
        )
        wide = jnp.concatenate([raw[:, 64:], jnp.zeros((TOK, 128), jnp.float32)], axis=1)
        queries = list(heads(wide, gains[0:1], mine))
        places_of = [(head, block) for head in range(3) for block in range(2)]
        scores, probs = [], []
        for head, block in places_of:
            window = pl.ds(pl.multiple_of(info[3 + block], BLOCK), 4 * BLOCK)
            scores.append(
                lax.dot_general(
                    queries[head][BLOCK * block : BLOCK * (block + 1)],
                    keys[3 * column_half + head, window],
                    (((1,), (1,)), ((), ())),
                    preferred_element_type=jnp.float32,
                )
            )
        column = lax.broadcasted_iota(jnp.int32, (1, 4 * BLOCK), 1)
        for (head, block), score in zip(places_of, scores):
            score = jnp.where(column < info[5 + block], score * (HEAD ** (-0.5)), -1e30)
            expo = jnp.exp(score - jnp.max(score, axis=1, keepdims=True))
            probs.append((expo * (1.0 / jnp.sum(expo, axis=1, keepdims=True))).astype(jnp.bfloat16))
        both = []
        for (head, block), prob in zip(places_of, probs):
            window = pl.ds(pl.multiple_of(info[3 + block], BLOCK), 4 * BLOCK)
            both.append(
                jnp.dot(prob, values[3 * column_half + head, window], preferred_element_type=jnp.float32)
            )
            if block == 1:
                mixed.append(jnp.concatenate(both, axis=0)[:, :HEAD])
                both = []
    out[...] = jnp.concatenate(mixed, axis=1).astype(jnp.bfloat16)


def attend(info, table, gains, spread, tokens_of, pieces):
    anywhere = pl.BlockSpec(memory_space=pl.ANY)
    vmem = pl.BlockSpec(memory_space=pltpu.VMEM)
    return pl.pallas_call(
        attend_kernel,
        out_shape=jax.ShapeDtypeStruct((TOK, 2 * THREE), jnp.bfloat16),
        in_specs=[pl.BlockSpec(memory_space=pltpu.SMEM), vmem, vmem, vmem] + [anywhere] * 13,
        out_specs=vmem,
        scratch_shapes=[
            pltpu.VMEM((2, D, 3 * THREE), jnp.bfloat16),
            pltpu.VMEM((WIN, D), jnp.bfloat16),
            pltpu.VMEM((6, WIN, LANES), jnp.bfloat16),
            pltpu.VMEM((6, WIN, LANES), jnp.bfloat16),
            pltpu.SemaphoreType.DMA((2,)),
            pltpu.SemaphoreType.DMA,
        ],
        compiler_params=pltpu.CompilerParams(vmem_limit_bytes=60 * 2**20),
        cost_estimate=pl.CostEstimate(
            flops=2 * D * 864 * 2 * 1024, bytes_accessed=14 * 2**20, transcendentals=2**20
        ),
    )(info, table, gains, spread, *tokens_of, *pieces)


def places(img_blocks, img_width, pack, shard):
    blocks = lax.dynamic_slice_in_dim(img_blocks, pack, 1, 0)[0]
    widths = lax.dynamic_slice_in_dim(img_width, pack, 1, 0)[0]
    order = jnp.arange(64, dtype=jnp.int32)
    starts = jnp.sum(jnp.where(order[None, :] < order[:, None], blocks[None, :], 0), axis=1)
    block_at = shard * 2 - 3 + jnp.arange(8, dtype=jnp.int32)
    begun = starts[None, :] <= block_at[:, None]
    inside = begun & (block_at[:, None] < (starts + blocks)[None, :])
    begin = jnp.sum(jnp.where(inside, starts[None, :], 0), axis=1)
    length = jnp.sum(jnp.where(inside, blocks[None, :], 0), axis=1)
    across = jnp.maximum(jnp.sum(jnp.where(inside, widths[None, :], 0), axis=1), 1)
    offset = (block_at - begin)[:, None] * BLOCK + jnp.arange(BLOCK, dtype=jnp.int32)[None, :]
    row, column = lax.div(offset, across[:, None] + 0 * offset), lax.rem(offset, across[:, None] + 0 * offset)
    back = (begin - block_at + jnp.arange(8, dtype=jnp.int32)) * BLOCK
    return row.reshape(WIN), column.reshape(WIN), back, length * BLOCK


def angles(row, column):
    lane = jnp.arange(LANES, dtype=jnp.int32)
    freq = 10000.0 ** (-(lane % 24).astype(jnp.float32) / 24)
    place = jnp.where(lane[None, :] < 48, row[:, None], column[:, None]).astype(jnp.float32)
    angle = place * freq[None, :]
    sign = jnp.where(lane % 48 < 24, -1.0, 1.0)
    real = lane < HEAD
    return jnp.stack(
        [jnp.where(real, jnp.cos(angle), 0.0), jnp.where(real, jnp.sin(angle) * sign, 0.0)]
    )


def spread_heads():
    feature, lane = jnp.arange(384)[:, None], jnp.arange(384)[None, :]
    return ((feature // HEAD == lane // LANES) & (feature < THREE)).astype(jnp.bfloat16)


def shards(tokens, norm_gain, w_qkv, q_gain, k_gain, img_blocks, img_width):
    xh, core, y, xl, z = (lax.axis_index(a) for a in AXES)
    shard = (y * 2 + xl) * 8 + z
    mine = jnp.concatenate([w_qkv[1], w_qkv[2], w_qkv[0]], axis=1)
    rows = gather_z(mine).reshape(2, 144, 3 * THREE)
    wide = tokens[0].astype(jnp.float32)
    scaled = wide * lax.rsqrt(jnp.mean(wide * wide, axis=-1, keepdims=True) + EPS) * norm_gain
    normed = scaled.astype(jnp.bfloat16)
    swap = functools.partial(move, where=along("c", 1))
    step_out, step_in = mirrored(along_seq, 1), mirrored(along_seq, -1)
    ring_out, ring_in = [mirrored(functools.partial(along, "z"), by) for by in (1, -1)]
    crossing = move(normed, across_ends)
    normed_other = swap(normed)
    gains = jnp.pad(jnp.stack([q_gain, k_gain]), ((0, 0), (0, LANES - HEAD)))
    mine_at = [places(img_blocks, img_width, pack, shard) for pack in (xh * 2 + 1 - core, xh * 2 + core)]
    tables = [angles(row, column) for row, column, _, _ in mine_at]
    rows, normed, normed_other, mine_at, tables = lax.optimization_barrier(
        (rows, normed, normed_other, mine_at, tables)
    )
    x_near, y_near = neighbours(rows[0], "x"), neighbours(rows[1], "y")
    x_near, y_near, crossing = lax.optimization_barrier((x_near, y_near, crossing))
    use_crossing = (z == jnp.where(core == 0, 7, 0)), (z == jnp.where(core == 0, 0, 7))
    side = move(jnp.where(use_crossing[0], crossing, normed), ring_out)
    first = jnp.stack([rows[0], *x_near, opposite(*x_near, "x", core)])
    second = jnp.stack([rows[1], *y_near, opposite(*y_near, "y", core)])
    first, second, normed, crossing = lax.optimization_barrier((first, second, normed, crossing))
    y_near, x_near = neighbours(first, "y"), neighbours(second, "x")
    back = move(jnp.where(use_crossing[1], crossing, normed), ring_in)
    side_other = swap(side)
    x_near, y_near = lax.optimization_barrier((x_near, y_near))
    x_far, y_far = opposite(*x_near, "x", core), opposite(*y_near, "y", core)
    x_near, y_near, side, back, side_other = lax.optimization_barrier((x_near, y_near, side, back, side_other))
    edge = TOK - BLOCK
    far_side = move(lax.dynamic_slice_in_dim(side, jnp.where(core == 0, edge, 0), BLOCK, 0), step_out)
    far_back = move(lax.dynamic_slice_in_dim(back, jnp.where(core == 0, 0, edge), BLOCK, 0), step_in)
    back_other = swap(back)
    tokens_here = (normed, side, back, far_side, far_back)
    far_other = swap(far_side), swap(far_back)

    def info(which, place):
        _, _, first_at, length = mine_at[which]
        scalars = jnp.stack([xh * 2 + xl, y, place]).astype(jnp.int32)
        return jnp.concatenate([scalars, first_at[3:5], length[3:5]])

    pieces = [first, *y_near, y_far, second, *x_near, x_far]
    ours = attend(info(1, core), tables[1], gains, spread_heads(), tokens_here, pieces)
    ours, far_other, back_other = lax.optimization_barrier((ours, far_other, back_other))
    tokens_other = (normed_other, side_other, back_other, *far_other)
    theirs = attend(info(0, 1 - core), tables[0], gains, spread_heads(), tokens_other, pieces)
    received = swap(theirs)
    left = jnp.where(core == 0, ours, received)
    right = jnp.where(core == 0, received, ours)
    whole = jnp.concatenate(
        [left[:, :THREE], right[:, :THREE], left[:, THREE:], right[:, THREE:]], axis=1
    )
    return whole[None]


def solution(mesh):
    devices = mesh.devices.reshape([SIZES[a] for a in AXES])
    fine = Mesh(devices, AXES)
    return jax.shard_map(
        shards,
        mesh=fine,
        in_specs=(
            P(("xh", "c"), ("y", "xl", "z"), None),
            P(),
            P(None, ("y", "xl", "z"), ("xh", "c")),
            P(),
            P(),
            P(),
            P(),
        ),
        out_specs=P(("xh", "c"), ("y", "xl", "z"), None),
        check_vma=False,
    )
```

```python
import functools
import itertools

import jax
import jax.numpy as jnp
from jax import lax
from jax.experimental import pallas as pl
from jax.experimental.pallas import tpu as pltpu
from jax.sharding import Mesh
from jax.sharding import PartitionSpec as P

HEAD = 96
BLOCK = 128
EPS = 1e-06
LANES = 128
AXES = ("xh", "c", "y", "xl", "z")
SIZES = {"xh": 2, "c": 2, "y": 4, "xl": 2, "z": 8}
D = 2304
TOK = 256
REACH = 3 * BLOCK
WIN = TOK + 2 * REACH
STEP = 256
THREE = 288
OTHERS = (1, -1, 2)


def move(value, where):
    pairs = []
    for place in itertools.product(*[range(SIZES[a]) for a in AXES]):
        target = where(dict(zip(AXES, place)))
        if target is None:
            continue
        source_at = target_at = 0
        for axis, coordinate in zip(AXES, place):
            source_at = source_at * SIZES[axis] + coordinate
            target_at = target_at * SIZES[axis] + target[axis]
        pairs.append((source_at, target_at))
    return lax.ppermute(value, AXES, pairs)


def along(axis, by):
    def where(place):
        if axis == "x":
            x = (place["xh"] * 2 + place["xl"] + by) % 4
            return {**place, "xh": x // 2, "xl": x % 2}
        return {**place, axis: (place[axis] + by) % SIZES[axis]}

    return where


def along_seq(by):
    def where(place):
        s = (place["y"] * 2 + place["xl"]) * 8 + place["z"] + by
        if not 0 <= s < 64:
            return None
        return {**place, "y": s // 16, "xl": s // 8 % 2, "z": s % 8}

    return where


def across_ends(place):
    if place["z"] not in (0, 7):
        return None
    target = along_seq(1 if place["z"] == 7 else -1)(place)
    return target and {**target, "z": place["z"]}


def mirrored(axis_move, by):
    def where(place):
        return axis_move(by if place["c"] == 0 else -by)(place)

    return where


def neighbours(value, axis):
    return move(value, along(axis, -1)), move(value, along(axis, 1))


def opposite(ahead, behind, axis, core):
    return move(jnp.where(core == 0, behind, ahead), mirrored(functools.partial(along, axis), 1))


def gather_z(mine, later):
    z = lax.axis_index("z")
    ahead, behind = move(mine, along("z", -1)), move(mine, along("z", 1))
    ahead, behind, later = lax.optimization_barrier((ahead, behind, later))
    three = jnp.stack([behind, mine, ahead])
    far_ahead, far_behind = move(three, along("z", -3)), move(three, along("z", 3))
    relative = jnp.concatenate([far_behind, three, far_ahead[:2]], axis=0)
    doubled = jnp.concatenate([relative, relative], axis=0)
    return lax.dynamic_slice_in_dim(doubled, (12 - z) % 8, 8, 0), later


def attend_kernel(info, table, gains, spread, *refs):
    tokens_of, pieces = refs[:5], refs[5:13]
    out, w_all, x_all, keys, values, w_sem, x_sem = refs[13:]
    x_here, y_here, flipped = info[0], info[1], info[2]
    left, right = BLOCK, REACH + TOK
    starts = (
        REACH,
        jnp.where(flipped == 0, left, right),
        jnp.where(flipped == 0, right, left),
        jnp.where(flipped == 0, 0, WIN - BLOCK),
        jnp.where(flipped == 0, WIN - BLOCK, 0),
    )
    for source, at in zip(tokens_of, starts):
        rows = pl.ds(pl.multiple_of(at, BLOCK), source.shape[0])
        pltpu.make_async_copy(source, x_all.at[rows], x_sem).start()

    def fetch(column_half):
        for half in range(2):
            for far in range(4):
                for near in range(4):
                    by_near, by_far = ((0,) + OTHERS)[near], ((0,) + OTHERS)[far]
                    dx, dy = (by_near, by_far) if half == 0 else (by_far, by_near)
                    x_from = lax.rem(x_here + (dx + 4), 4)
                    y_from = lax.rem(y_here + (dy + 4), 4)
                    row = (2 * y_from + lax.rem(x_from, 2)) * 288 + half * 144
                    rows = pl.ds(pl.multiple_of(row, 144), 144)

                    @pl.when(lax.div(x_from, 2) == column_half)
                    def _():
                        pltpu.make_async_copy(
                            pieces[4 * half + far].at[near], w_all.at[column_half, rows], w_sem.at[column_half]
                        ).start()

    fetch(0)
    fetch(1)
    pltpu.make_async_copy(x_all, x_all, x_sem).wait()
    low = lax.rem(lax.broadcasted_iota(jnp.int32, (1, LANES), 1), 48) < 24

    def unit(wide):
        square = wide * wide
        high = square.astype(jnp.bfloat16)
        rest = (square - high.astype(jnp.float32)).astype(jnp.bfloat16)
        total = jnp.dot(high, spread[...], preferred_element_type=jnp.float32)
        total = total + jnp.dot(rest, spread[...], preferred_element_type=jnp.float32)
        return lax.rsqrt(total * (1.0 / HEAD) + EPS)

    def turn(value, cosine, sine):
        partner = jnp.where(low, pltpu.roll(value, LANES - 24, 1), pltpu.roll(value, 24, 1))
        return value * cosine + partner * sine

    def heads(wide, gain, rows):
        scale = unit(wide[:, :384])
        cosine, sine = table[0, rows], table[1, rows]
        for head in range(3):
            part = wide[:, HEAD * head : HEAD * head + LANES] * scale[:, LANES * head : LANES * (head + 1)]
            yield turn(part * gain, cosine, sine).astype(jnp.bfloat16)

    mixed = []
    for column_half in range(2):
        pltpu.make_async_copy(
            w_all.at[column_half], w_all.at[column_half], w_sem.at[column_half]
        ).wait()
        for step in range(WIN // STEP):
            rows = pl.ds(step * STEP, STEP)
            raw = jnp.dot(
                x_all[rows], w_all[column_half, :, 0:640], preferred_element_type=jnp.float32
            )
            for head, turned in enumerate(heads(raw, gains[1:2], rows)):
                keys[3 * column_half + head, rows] = turned
            for head in range(3):
                part = raw[:, THREE + HEAD * head : THREE + HEAD * head + LANES]
                values[3 * column_half + head, rows] = part.astype(jnp.bfloat16)
        mine = pl.ds(REACH, TOK)
        raw = jnp.dot(
            x_all[mine], w_all[column_half, :, 512:864], preferred_element_type=jnp.float32
        )
        wide = jnp.concatenate([raw[:, 64:], jnp.zeros((TOK, 128), jnp.float32)], axis=1)
        queries = list(heads(wide, gains[0:1], mine))
        places_of = [(head, block) for head in range(3) for block in range(2)]
        scores, probs = [], []
        for head, block in places_of:
            window = pl.ds(pl.multiple_of(info[3 + block], BLOCK), 4 * BLOCK)
            scores.append(
                lax.dot_general(
                    queries[head][BLOCK * block : BLOCK * (block + 1)],
                    keys[3 * column_half + head, window],
                    (((1,), (1,)), ((), ())),
                    preferred_element_type=jnp.float32,
                )
            )
        column = lax.broadcasted_iota(jnp.int32, (1, 4 * BLOCK), 1)
        for (head, block), score in zip(places_of, scores):
            score = jnp.where(column < info[5 + block], score * (HEAD ** (-0.5)), -1e30)
            expo = jnp.exp(score - jnp.max(score, axis=1, keepdims=True))
            probs.append((expo * (1.0 / jnp.sum(expo, axis=1, keepdims=True))).astype(jnp.bfloat16))
        both = []
        for (head, block), prob in zip(places_of, probs):
            window = pl.ds(pl.multiple_of(info[3 + block], BLOCK), 4 * BLOCK)
            both.append(
                jnp.dot(prob, values[3 * column_half + head, window], preferred_element_type=jnp.float32)
            )
            if block == 1:
                mixed.append(jnp.concatenate(both, axis=0)[:, :HEAD])
                both = []
    out[...] = jnp.concatenate(mixed, axis=1).astype(jnp.bfloat16)


def attend(info, table, gains, spread, tokens_of, pieces):
    anywhere = pl.BlockSpec(memory_space=pl.ANY)
    vmem = pl.BlockSpec(memory_space=pltpu.VMEM)
    return pl.pallas_call(
        attend_kernel,
        out_shape=jax.ShapeDtypeStruct((TOK, 2 * THREE), jnp.bfloat16),
        in_specs=[pl.BlockSpec(memory_space=pltpu.SMEM), vmem, vmem, vmem] + [anywhere] * 13,
        out_specs=vmem,
        scratch_shapes=[
            pltpu.VMEM((2, D, 3 * THREE), jnp.bfloat16),
            pltpu.VMEM((WIN, D), jnp.bfloat16),
            pltpu.VMEM((6, WIN, LANES), jnp.bfloat16),
            pltpu.VMEM((6, WIN, LANES), jnp.bfloat16),
            pltpu.SemaphoreType.DMA((2,)),
            pltpu.SemaphoreType.DMA,
        ],
        compiler_params=pltpu.CompilerParams(vmem_limit_bytes=60 * 2**20),
        cost_estimate=pl.CostEstimate(
            flops=2 * D * 864 * 2 * 1024, bytes_accessed=14 * 2**20, transcendentals=2**20
        ),
    )(info, table, gains, spread, *tokens_of, *pieces)


def places(img_blocks, img_width, pack, shard):
    blocks = lax.dynamic_slice_in_dim(img_blocks, pack, 1, 0)[0]
    widths = lax.dynamic_slice_in_dim(img_width, pack, 1, 0)[0]
    order = jnp.arange(64, dtype=jnp.int32)
    starts = jnp.sum(jnp.where(order[None, :] < order[:, None], blocks[None, :], 0), axis=1)
    block_at = shard * 2 - 3 + jnp.arange(8, dtype=jnp.int32)
    begun = starts[None, :] <= block_at[:, None]
    inside = begun & (block_at[:, None] < (starts + blocks)[None, :])
    begin = jnp.sum(jnp.where(inside, starts[None, :], 0), axis=1)
    length = jnp.sum(jnp.where(inside, blocks[None, :], 0), axis=1)
    across = jnp.maximum(jnp.sum(jnp.where(inside, widths[None, :], 0), axis=1), 1)
    offset = (block_at - begin)[:, None] * BLOCK + jnp.arange(BLOCK, dtype=jnp.int32)[None, :]
    row, column = lax.div(offset, across[:, None] + 0 * offset), lax.rem(offset, across[:, None] + 0 * offset)
    back = (begin - block_at + jnp.arange(8, dtype=jnp.int32)) * BLOCK
    return row.reshape(WIN), column.reshape(WIN), back, length * BLOCK


def angles(row, column):
    lane = jnp.arange(LANES, dtype=jnp.int32)
    freq = 10000.0 ** (-(lane % 24).astype(jnp.float32) / 24)
    place = jnp.where(lane[None, :] < 48, row[:, None], column[:, None]).astype(jnp.float32)
    angle = place * freq[None, :]
    sign = jnp.where(lane % 48 < 24, -1.0, 1.0)
    real = lane < HEAD
    return jnp.stack(
        [jnp.where(real, jnp.cos(angle), 0.0), jnp.where(real, jnp.sin(angle) * sign, 0.0)]
    )


def spread_heads():
    feature, lane = jnp.arange(384)[:, None], jnp.arange(384)[None, :]
    return ((feature // HEAD == lane // LANES) & (feature < THREE)).astype(jnp.bfloat16)


def shards(tokens, norm_gain, w_qkv, q_gain, k_gain, img_blocks, img_width):
    xh, core, y, xl, z = (lax.axis_index(a) for a in AXES)
    shard = (y * 2 + xl) * 8 + z
    mine = jnp.concatenate([w_qkv[1], w_qkv[2], w_qkv[0]], axis=1)
    mine_at = [places(img_blocks, img_width, pack, shard) for pack in (xh * 2 + 1 - core, xh * 2 + core)]
    rows, mine_at = gather_z(mine, mine_at)
    rows = rows.reshape(2, 144, 3 * THREE)
    wide = tokens[0].astype(jnp.float32)
    scaled = wide * lax.rsqrt(jnp.mean(wide * wide, axis=-1, keepdims=True) + EPS) * norm_gain
    normed = scaled.astype(jnp.bfloat16)
    swap = functools.partial(move, where=along("c", 1))
    step_out, step_in = mirrored(along_seq, 1), mirrored(along_seq, -1)
    ring_out, ring_in = [mirrored(functools.partial(along, "z"), by) for by in (1, -1)]
    crossing = move(normed, across_ends)
    normed_other = swap(normed)
    gains = jnp.pad(jnp.stack([q_gain, k_gain]), ((0, 0), (0, LANES - HEAD)))
    tables = [angles(row, column) for row, column, _, _ in mine_at]
    rows, normed, normed_other, mine_at, tables = lax.optimization_barrier(
        (rows, normed, normed_other, mine_at, tables)
    )
    x_near, y_near = neighbours(rows[0], "x"), neighbours(rows[1], "y")
    x_near, y_near, crossing = lax.optimization_barrier((x_near, y_near, crossing))
    use_crossing = (z == jnp.where(core == 0, 7, 0)), (z == jnp.where(core == 0, 0, 7))
    side = move(jnp.where(use_crossing[0], crossing, normed), ring_out)
    first = jnp.stack([rows[0], *x_near, opposite(*x_near, "x", core)])
    second = jnp.stack([rows[1], *y_near, opposite(*y_near, "y", core)])
    first, second, normed, crossing = lax.optimization_barrier((first, second, normed, crossing))
    y_near, x_near = neighbours(first, "y"), neighbours(second, "x")
    back = move(jnp.where(use_crossing[1], crossing, normed), ring_in)
    side_other = swap(side)
    edge = TOK - BLOCK
    side_edge = lax.dynamic_slice_in_dim(side, jnp.where(core == 0, edge, 0), BLOCK, 0)
    x_near, y_near, side_edge = lax.optimization_barrier((x_near, y_near, side_edge))
    x_far, y_far = opposite(*x_near, "x", core), opposite(*y_near, "y", core)
    far_side = move(side_edge, step_out)
    x_near, y_near, back, side_other = lax.optimization_barrier((x_near, y_near, back, side_other))
    far_back = move(lax.dynamic_slice_in_dim(back, jnp.where(core == 0, 0, edge), BLOCK, 0), step_in)
    back_other = swap(back)
    tokens_here = (normed, side, back, far_side, far_back)
    far_other = swap(far_side), swap(far_back)

    def info(which, place):
        _, _, first_at, length = mine_at[which]
        scalars = jnp.stack([xh * 2 + xl, y, place]).astype(jnp.int32)
        return jnp.concatenate([scalars, first_at[3:5], length[3:5]])

    pieces = [first, *y_near, y_far, second, *x_near, x_far]
    ours = attend(info(1, core), tables[1], gains, spread_heads(), tokens_here, pieces)
    ours, far_other, back_other = lax.optimization_barrier((ours, far_other, back_other))
    tokens_other = (normed_other, side_other, back_other, *far_other)
    theirs = attend(info(0, 1 - core), tables[0], gains, spread_heads(), tokens_other, pieces)
    received = swap(theirs)
    left = jnp.where(core == 0, ours, received)
    right = jnp.where(core == 0, received, ours)
    whole = jnp.concatenate(
        [left[:, :THREE], right[:, :THREE], left[:, THREE:], right[:, THREE:]], axis=1
    )
    return whole[None]


def solution(mesh):
    devices = mesh.devices.reshape([SIZES[a] for a in AXES])
    fine = Mesh(devices, AXES)
    return jax.shard_map(
        shards,
        mesh=fine,
        in_specs=(
            P(("xh", "c"), ("y", "xl", "z"), None),
            P(),
            P(None, ("y", "xl", "z"), ("xh", "c")),
            P(),
            P(),
            P(),
            P(),
        ),
        out_specs=P(("xh", "c"), ("y", "xl", "z"), None),
        check_vma=False,
    )
```
